256 devices in a mesh: lon: 64 (over x_lo, y, z), lat: 4 (over x_hi, core).
Axes of the slice: x: 4 (x_hi: 2, x_lo: 2; x = x_hi * 2 + x_lo), y: 4, z: 8, core: 2. Of those that a mesh axis runs over, the one named last changes fastest.
Arguments:
- air_state: bfloat16 [8, 48, 768, 192], P(None, 'lat', 'lon'), may hold values from -6 to 6
- cotangent: bfloat16 [8, 48, 768, 192], P(None, 'lat', 'lon'), may hold values from -6 to 6
- norm_gain: float32 [192], replicated, may hold values from 0.1 to 1.9
- norm_shift: float32 [192], replicated, may hold values from -3 to 3
- qkv_weight: bfloat16 [192, 576], replicated, may hold values from -0.4375 to 0.4375
- proj_weight: bfloat16 [192, 192], replicated, may hold values from -0.4375 to 0.4375
- earth_bias: float32 [8, 4, 6, 3312], P('lat'), may hold values from -4.5 to 250
Outputs:
- air_out: bfloat16 [8, 48, 768, 192], P(None, 'lat', 'lon')
- state_grad: bfloat16 [8, 48, 768, 192], P(None, 'lat', 'lon')
- qkv_grad: float32 [192, 576], replicated
- proj_grad: float32 [192, 192], replicated
- gain_grad: float32 [192], replicated
- shift_grad: float32 [192], replicated
- bias_grad: bfloat16 [8, 4, 6, 3312], P('lat')
The draws below stay inside these ranges and needn't reach their ends.
All inputs are finite; a program needn't handle non-finite values.
Results may differ from the reference program's by a relative error of at most 0.01.
Values may be sent and summed in bfloat16 or wider, within the bound.
No kernel may reach another device: no remote copies, remote signals or barrier semaphores. Data moves between devices by JAX's collectives and lax.ppermute only.
A program may use at most 128 MiB of HBM per device.

```python
import math
import jax
import jax.numpy as jnp
import numpy as np
from jax import lax

C = 192
HEADS = 6
LEVELS = 8
WZ = 2
WLAT = 6
WLON = 12
NLAT = 48
NLON = 768
TOKENS = 294912
LATWIN = 8
ZWIN = 4
WTOK = 144
POSITIONS = 3312


def draw_earth_bias(key, part):
    key = jax.random.fold_in(key, 11)
    key_base = jax.random.fold_in(key, 0)
    full_shape = (LATWIN, ZWIN, HEADS, POSITIONS)
    return jnp.clip(jax.random.normal(key_base, full_shape, jnp.float32), -4.5, 4.5)


def level_of(rng, dims, shards, smallest, high):
    gain, own = 1.0, jax.random.fold_in(rng, 6)
    for dim, blocks in shards:
        heights = jnp.exp(jax.random.uniform(jax.random.fold_in(own, dim), (blocks,), jnp.float32, smallest / len(shards), high / len(shards)))
        gain = gain * jnp.repeat(heights, dims[dim] // blocks).reshape([-1 if axis == dim else 1 for axis in range(len(dims))])
    return gain


def scatter_about(own_key, extent, spread, limit, cuts=(), kind=jnp.bfloat16):
    entries = spread * jax.random.normal(own_key, extent, jnp.float32)
    if cuts:
        entries = entries * level_of(own_key, extent, cuts, -0.22, 0.18)
    return jnp.clip(entries, -limit, limit).astype(kind)


def setup_inputs(seed: int = 0) -> dict:
    key_of = jax.random.split(jax.random.key(seed), 8)
    return {
        "air_state": scatter_about(key_of[0], (LEVELS, NLAT, NLON, C), 1.0, 6.0, ((1, 4), (2, 64))),
        "cotangent": scatter_about(key_of[1], (LEVELS, NLAT, NLON, C), 1.0, 6.0, ((1, 4), (2, 64))),
        "norm_gain": jnp.clip(1.0 + 0.18 * jax.random.normal(key_of[2], (C,), jnp.float32), 0.1, 1.9),
        "norm_shift": scatter_about(key_of[3], (C,), 0.5, 3.0, (), jnp.float32),
        "qkv_weight": scatter_about(key_of[4], (C, 3 * C), C ** -0.5, 0.4375),
        "proj_weight": scatter_about(key_of[5], (C, C), C ** -0.5, 0.4375),
        "earth_bias": draw_earth_bias(jax.random.fold_in(key_of[7], 71), 0),
    }


EPSILON = 1e-05
MASKED = -1e+30

def window_layout():
    level_pos, row_pos, col_pos = np.meshgrid(np.arange(WZ), np.arange(WLAT), np.arange(WLON), indexing='ij')
    level_pos = level_pos.reshape(-1)
    row_pos = row_pos.reshape(-1)
    col_pos = col_pos.reshape(-1)
    position = ((level_pos[:, None] * WZ + level_pos[None, :]) * (WLAT * WLAT) + row_pos[:, None] * WLAT + row_pos[None, :]) * (2 * WLON - 1) + col_pos[:, None] - col_pos[None, :] + WLON - 1
    return (level_pos.astype(np.int32), row_pos.astype(np.int32), col_pos.astype(np.int32), position.reshape(-1).astype(np.int32))

def fold_positions(grads, position):
    leading = grads.shape[:-2]
    flat_rows = grads.reshape(-1, grads.shape[-1] * grads.shape[-1])
    folded = jax.ops.segment_sum(flat_rows.T, jnp.asarray(position), num_segments=POSITIONS)
    return folded.T.reshape(leading + (POSITIONS,))

def region_codes(lat_ids, z_id, level_pos, row_pos):
    lat_side = (lat_ids[:, None] * WLAT + row_pos[None, :] < WLAT // 2).astype(jnp.int32)
    level_side = (z_id * WZ + level_pos < WZ // 2).astype(jnp.int32)
    region_code = lat_side * 2 + level_side[None, :]
    return region_code[:, :, None] == region_code[:, None, :]

def mixed_product(form, left, right):
    return jnp.einsum(form, left.astype(jnp.float32), right.astype(jnp.float32))

def layer_terms(state_win, upstream, norm_gain, norm_shift, qkv_weight, proj_weight, bias_full, allowed):
    win_count, tokens_win, channels = state_win.shape
    head_dim = channels // HEADS
    score_scale = head_dim ** (-0.5)
    state_float = state_win.astype(jnp.float32)
    row_mean = lax.optimization_barrier(jnp.mean(state_float, axis=-1, keepdims=True))
    centred = state_float - row_mean
    inv_std = lax.rsqrt(lax.optimization_barrier(jnp.mean(centred * centred, axis=-1, keepdims=True)) + EPSILON)
    standard = centred * inv_std
    normed = (standard * norm_gain + norm_shift).astype(jnp.bfloat16)
    projected = mixed_product('wpc,cf->wpf', normed, qkv_weight).astype(jnp.bfloat16)
    split_heads = projected.reshape(win_count, tokens_win, 3, HEADS, head_dim)
    queries = split_heads[:, :, 0]
    key_rows = split_heads[:, :, 1]
    value_rows = split_heads[:, :, 2]
    scores = mixed_product('wqhd,wkhd->whqk', queries, key_rows) * score_scale + bias_full
    scores = jnp.where(allowed[:, None], scores, MASKED)
    row_max = lax.optimization_barrier(jnp.max(scores, axis=-1, keepdims=True))
    exponent = jnp.exp(scores - row_max)
    attn_probs = exponent / lax.optimization_barrier(jnp.sum(exponent, axis=-1, keepdims=True))
    probs_half = attn_probs.astype(jnp.bfloat16)
    context = mixed_product('whqk,wkhd->wqhd', probs_half, value_rows).astype(jnp.bfloat16).reshape(win_count, tokens_win, channels)
    attended = mixed_product('wpc,cd->wpd', context, proj_weight)
    out_win = (state_float + attended).astype(jnp.bfloat16)
    ctx_grad = mixed_product('wpd,cd->wpc', upstream, proj_weight).astype(jnp.bfloat16)
    proj_part = mixed_product('wpc,wpd->cd', context, upstream)
    ctx_heads = ctx_grad.reshape(win_count, tokens_win, HEADS, head_dim)
    probs_grad = mixed_product('wqhd,wkhd->whqk', ctx_heads, value_rows)
    value_grad = mixed_product('whqk,wqhd->wkhd', probs_half, ctx_heads)
    row_dot = lax.optimization_barrier(jnp.sum(probs_grad * attn_probs, axis=-1, keepdims=True))
    score_grad = attn_probs * (probs_grad - row_dot)
    scaled_grad = (score_grad * score_scale).astype(jnp.bfloat16)
    query_grad = mixed_product('whqk,wkhd->wqhd', scaled_grad, key_rows)
    key_grad = mixed_product('whqk,wqhd->wkhd', scaled_grad, queries)
    qkv_rows_grad = jnp.stack((query_grad, key_grad, value_grad), axis=2).reshape(win_count, tokens_win, 3 * channels).astype(jnp.bfloat16)
    qkv_part = mixed_product('wpc,wpf->cf', normed, qkv_rows_grad)
    normed_grad = mixed_product('wpf,cf->wpc', qkv_rows_grad, qkv_weight)
    gain_part = lax.optimization_barrier(jnp.sum(normed_grad * standard, axis=(0, 1)))
    shift_part = lax.optimization_barrier(jnp.sum(normed_grad, axis=(0, 1)))
    scaled = normed_grad * norm_gain
    branch_grad = inv_std * (scaled - lax.optimization_barrier(jnp.mean(scaled, axis=-1, keepdims=True)) - standard * lax.optimization_barrier(jnp.mean(scaled * standard, axis=-1, keepdims=True)))
    grad_win = (upstream.astype(jnp.float32) + branch_grad).astype(jnp.bfloat16)
    return (out_win, grad_win, score_grad, (qkv_part, proj_part, gain_part, shift_part))

def reference(air_state, cotangent, norm_gain, norm_shift, qkv_weight, proj_weight, earth_bias):
    level_pos, row_pos, col_pos, position = window_layout()
    roll_steps = (WZ // 2, WLAT // 2, WLON // 2)
    back_steps = (-(WZ // 2), -(WLAT // 2), -(WLON // 2))
    lon_windows = NLON // WLON

    def cut_windows(grid):
        shaped = grid.reshape(ZWIN, WZ, LATWIN, WLAT, lon_windows, WLON, C).transpose(0, 2, 4, 1, 3, 5, 6)
        return shaped.reshape(ZWIN * LATWIN, lon_windows, WTOK, C)

    def join_windows(windows):
        shaped = windows.reshape(ZWIN, LATWIN, lon_windows, WZ, WLAT, WLON, C).transpose(0, 3, 1, 4, 2, 5, 6)
        return jnp.roll(shaped.reshape(LEVELS, NLAT, NLON, C), back_steps, axis=(0, 1, 2))
    state_windows = cut_windows(jnp.roll(air_state, roll_steps, axis=(0, 1, 2)))
    upstream_windows = cut_windows(jnp.roll(cotangent, roll_steps, axis=(0, 1, 2)))
    z_ids = jnp.repeat(jnp.arange(ZWIN, dtype=jnp.int32), LATWIN)
    lat_ids = jnp.tile(jnp.arange(LATWIN, dtype=jnp.int32), ZWIN)
    flat_index = jnp.asarray(position)
    level_table = jnp.asarray(level_pos)
    row_table = jnp.asarray(row_pos)

    def block_step(running, inputs):
        state_win, upstream, z_id, lat_id = inputs
        bias_table = earth_bias[lat_id, z_id]
        bias_full = jnp.take(bias_table, flat_index, axis=1).reshape(1, HEADS, WTOK, WTOK)
        allowed = region_codes(lat_id[None], z_id, level_table, row_table)
        out_win, grad_win, score_grad, grad_parts = layer_terms(state_win, upstream, norm_gain, norm_shift, qkv_weight, proj_weight, bias_full, allowed)
        table_grad = fold_positions(lax.optimization_barrier(jnp.sum(score_grad, axis=0)), position)
        return (jax.tree.map(jnp.add, running, grad_parts), (out_win, grad_win, table_grad))
    start_sums = (jnp.zeros((C, 3 * C), jnp.float32), jnp.zeros((C, C), jnp.float32), jnp.zeros((C,), jnp.float32), jnp.zeros((C,), jnp.float32))
    totals, (out_windows, grad_windows, table_grads) = lax.scan(block_step, start_sums, (state_windows, upstream_windows, z_ids, lat_ids))
    grad_scale = 1.0 / math.sqrt(TOKENS)
    bias_grad = table_grads.reshape(ZWIN, LATWIN, HEADS, POSITIONS).transpose(1, 0, 2, 3).astype(jnp.bfloat16)
    return (join_windows(out_windows), join_windows(grad_windows), totals[0] * grad_scale, totals[1] * grad_scale, totals[2] * grad_scale, totals[3] * grad_scale, bias_grad)
```

```python
import functools
import math

import jax
import jax.numpy as jnp
import numpy as np
from jax import lax
from jax.experimental import pallas as pl
from jax.experimental.pallas import tpu as pltpu
from jax.sharding import Mesh, PartitionSpec as P

HEADS=6; WZ=2; WLAT=6; WLON=12; WTOK=144; POSITIONS=3312
C=192; HD=32
EPSILON=1e-5
MASKED=-1e30
QP=896
GL=72
F32=jnp.float32; BF16=jnp.bfloat16
SCALE=HD**-0.5

def nn(a,b): return lax.dot_general(a,b,(((1,),(0,)),((),())),preferred_element_type=F32)
def nt(a,b): return lax.dot_general(a,b,(((1,),(1,)),((),())),preferred_element_type=F32)
def tn(a,b): return lax.dot_general(a,b,(((0,),(0,)),((),())),preferred_element_type=F32)

def tile_groups(t):
    out=[]
    for g in range(12):
        lo=max(GL*g-128*t,0); hi=min(GL*(g+1)-128*t,128)
        if lo<hi: out.append((g,lo,hi))
    return out

def window(w, x_ref,u_ref,gain,shift,wq,wk,wv,wkT,wvT,wp,bias_ref,
           out_ref,grad_ref,fold_ref, s_scr,dp_scr,ph_scr,ds_scr,fold_scr, normed_scr,gq_scr,gk_scr,gv_scr,ctx_scr,up_scr,
           eye144, base):
    x=x_ref[0,w].astype(F32)
    u=u_ref[0,w]
    mean=jnp.mean(x,axis=-1,keepdims=True)
    cen=x-mean
    inv=lax.rsqrt(jnp.mean(cen*cen,axis=-1,keepdims=True)+EPSILON)
    std=cen*inv
    normed=(std*gain+shift).astype(BF16)
    q=nn(normed,wq).astype(BF16)
    k=nn(normed,wk).astype(BF16)
    v=nn(normed,wv).astype(BF16)
    kT=nt(wkT,normed).astype(BF16)
    vT=nt(wvT,normed).astype(BF16)
    dctx=nt(u,wp).astype(BF16)
    lane_c=lax.broadcasted_iota(jnp.int32,(1,C),1)//HD
    def blocks(m):
        zero=jnp.zeros_like(m)
        parts=[jnp.where(lane_c==h,m,zero) for h in range(HEADS)]
        return jnp.concatenate(parts+[jnp.zeros((QP-HEADS*WTOK,C),BF16)],axis=0)
    qblk=blocks(q); dblk=blocks(dctx)
    s_scr[w]=nt(k,qblk)
    dp_scr[w]=nt(v,dblk)
    lane=lax.broadcasted_iota(jnp.int32,(24,128),1)
    acc={}
    for t in range(7):
        groups=tile_groups(t)
        rows=[]
        for zk in range(WZ):
            for j in range(3):
                tile=None
                for (g,lo,hi) in groups:
                    h,zq=g//2,g%2
                    shift_=(GL*g-128*t-24*(2-j))%128
                    piece=bias_ref[w,0,h,zq,zk]
                    if shift_: piece=pltpu.roll(piece,shift_,1)
                    tile=piece if tile is None else jnp.where(lane>=lo,piece,tile)
                if groups[-1][2]<128: tile=jnp.where(lane<groups[-1][2],tile,0.0)
                rows.append(tile)
        bias=jnp.concatenate(rows,axis=0)
        cols=slice(128*t,128*(t+1))
        s=s_scr[w,:,cols]*SCALE+bias
        m=jnp.max(s,axis=0,keepdims=True)
        e=jnp.exp(s-m)
        p=e*(1.0/jnp.sum(e,axis=0,keepdims=True))
        ph_scr[w,:,cols]=p.astype(BF16)
        dp=dp_scr[w,:,cols]
        ds=p*(dp-jnp.sum(p*dp,axis=0,keepdims=True))
        ds_scr[w,:,cols]=(ds*SCALE).astype(BF16)
        for zk in range(WZ):
            for (g,lo,hi) in groups:
                tot=None
                for j in range(3):
                    r0=zk*72+24*j
                    piece=ds[r0:r0+24]
                    if lo>0 or hi<128:
                        piece=jnp.where((lane>=lo)&(lane<hi),piece,0.0)
                    back=(-(GL*g-128*t-24*(2-j)))%128
                    if back: piece=pltpu.roll(piece,back,1)
                    tot=piece if tot is None else tot+piece
                h,zq=g//2,g%2
                if GL*g-128*t>=0:
                    fold_scr[w,h,zq,zk]=tot
                else:
                    fold_scr[w,h,zq,zk]+=tot
    for h in range(HEADS):
        for zq in range(WZ):
            for zk in range(WZ):
                f=fold_scr[w,h,zq,zk]
                lo_t=None; hi_t=None
                lane6=lax.broadcasted_iota(jnp.int32,(8,128),1)
                for dw in range(4):
                    part=jnp.concatenate([f[6*dw:6*dw+6],jnp.zeros((2,128),F32)],axis=0)
                    sh=18-6*dw
                    r=pltpu.roll(part,sh,1) if sh else part
                    a=jnp.where(lane6>=sh,r,0.0) if sh>8 else r
                    lo_t=a if lo_t is None else lo_t+a
                    if sh>8:
                        b=jnp.where(lane6<sh-8,r,0.0)
                        hi_t=b if hi_t is None else hi_t+b
                tail=jnp.sum(pltpu.roll(hi_t,0,1,stride=10,stride_axis=0),axis=0,keepdims=True)
                n=(h*WZ+zq)*WZ+zk
                fold_ref[w,0,n//3,7*(n%3):7*(n%3)+7]=jnp.concatenate([lo_t[:6],tail],axis=0)
    ph=ph_scr[w]; dsc=ds_scr[w]
    ctxT=jnp.concatenate([nn(vT[32*h:32*h+32],ph[:,128*h:128*h+256])[:,16*h:16*h+WTOK] for h in range(HEADS)],axis=0).astype(BF16)
    dqT=jnp.concatenate([nn(kT[32*h:32*h+32],dsc[:,128*h:128*h+256])[:,16*h:16*h+WTOK] for h in range(HEADS)],axis=0).astype(BF16)
    ctx=nt(eye144,ctxT).astype(BF16)
    dq=nt(eye144,dqT).astype(BF16)
    dv=nn(ph,dblk).astype(BF16)
    dk=nn(dsc,qblk).astype(BF16)
    out_ref[0,w]=(x+nn(ctx,wp)).astype(BF16)
    ng=nt(dq,wq)+nt(dk,wk)+nt(dv,wv)
    g=ng*gain
    br=inv*(g-jnp.mean(g,axis=-1,keepdims=True)-std*jnp.mean(g*std,axis=-1,keepdims=True))
    grad_ref[0,w]=(u.astype(F32)+br).astype(BF16)
    rows=pl.ds(base+w*WTOK,WTOK)
    normed_scr[rows]=normed; gq_scr[rows]=dq; gk_scr[rows]=dk; gv_scr[rows]=dv; ctx_scr[rows]=ctx; up_scr[rows]=u
    return jnp.sum(ng*std,axis=0,keepdims=True), jnp.sum(ng,axis=0,keepdims=True)

def kernel(x_ref,u_ref,gain_ref,shift_ref,wq_ref,wk_ref,wv_ref,wkT_ref,wvT_ref,wp_ref,bias_ref,
           out_ref,grad_ref,fold_ref,wgrad_ref,*scr):
    ngrad_scr=scr[-1]; scr=scr[:-1]
    step=pl.program_id(0)
    eye=(lax.broadcasted_iota(jnp.int32,(WTOK,WTOK),0)==lax.broadcasted_iota(jnp.int32,(WTOK,WTOK),1)).astype(BF16)
    base=pl.multiple_of(step*2*WTOK,2*WTOK)
    gs=[]
    for w in range(2):
        gs.append(window(w,x_ref,u_ref,gain_ref[...],shift_ref[...],wq_ref[...],wk_ref[...],wv_ref[...],wkT_ref[...],wvT_ref[...],wp_ref[...],bias_ref,
            out_ref,grad_ref,fold_ref,*scr[:-1],eye,base))
    both=jnp.concatenate([gs[0][0]+gs[1][0],gs[0][1]+gs[1][1],jnp.zeros((6,C),F32)],axis=0)
    @pl.when(step==0)
    def _(): ngrad_scr[...]=both
    @pl.when(step>0)
    def _(): ngrad_scr[...]+=both
    @pl.when(step==pl.num_programs(0)-1)
    def _():
        normed_scr,gq_scr,gk_scr,gv_scr,ctx_scr,up_scr,w_scr=scr[5:]
        n=normed_scr[...]
        whole=jnp.concatenate([tn(n,gq_scr[...]),tn(n,gk_scr[...]),tn(n,gv_scr[...]),tn(ctx_scr[...],up_scr[...])],axis=1)
        for t in range(6):
            w_scr[C*t:C*(t+1)]=whole[:,128*t:128*(t+1)]
        for r in range(3):
            for t in range(6):
                m=r*6+t
                wgrad_ref[pl.ds((m//9)*64*16+m%9,64,stride=16),:]=w_scr[pl.ds(C*t+r,64,stride=3),:]
        ng=ngrad_scr[...]
        for half in range(2):
            wgrad_ref[pl.ds(half*64*16+9,64,stride=16),:]=jnp.broadcast_to(ng[half:half+1,:128],(64,128))
            wgrad_ref[pl.ds(half*64*16+10,64,stride=16),:]=jnp.broadcast_to(jnp.concatenate([ng[half:half+1,128:],jnp.zeros((1,64),F32)],axis=1),(64,128))

def attend(xw,uw,gain,shift,wqkv,wp,vtab):
    wq,wk,wv=wqkv[:,:C],wqkv[:,C:2*C],wqkv[:,2*C:]
    n=xw.shape[0]
    full=lambda *s: pl.BlockSpec(s,lambda i:(0,)*len(s))
    win=pl.BlockSpec((1,2,WTOK,C),lambda i:(i,0,0,0))
    tok=n*2*WTOK
    return pl.pallas_call(
        kernel,
        grid=(n,),
        in_specs=[win,win,full(1,C),full(1,C)]+[full(C,C)]*6+[pl.BlockSpec((2,1,HEADS,WZ,WZ,24,128),lambda i:(0,i,0,0,0,0,0))],
        out_specs=[win,win,pl.BlockSpec((2,1,8,24,128),lambda i:(0,i,0,0,0)),full(2*64*16,128)],
        out_shape=[jax.ShapeDtypeStruct(xw.shape,BF16),jax.ShapeDtypeStruct(xw.shape,BF16),
                   jax.ShapeDtypeStruct((2,n,8,24,128),F32),
                   jax.ShapeDtypeStruct((2*64*16,128),F32)],
        scratch_shapes=[pltpu.VMEM((2,WTOK,QP),F32),pltpu.VMEM((2,WTOK,QP),F32),pltpu.VMEM((2,WTOK,QP),BF16),pltpu.VMEM((2,WTOK,QP),BF16),
                        pltpu.VMEM((2,HEADS,WZ,WZ,24,128),F32)]+[pltpu.VMEM((tok,C),BF16)]*6+[pltpu.VMEM((6*C,128),F32),pltpu.VMEM((8,C),F32)],
        compiler_params=pltpu.CompilerParams(dimension_semantics=("arbitrary",),vmem_limit_bytes=48*1024*1024),
        name="attend",
    )(xw,uw,gain.reshape(1,C),shift.reshape(1,C),wq,wk,wv,wk.T,wv.T,wp,vtab)

def spread_table(earth_bias, lat0):
    a,b=earth_bias.shape[:2]
    t=earth_bias.reshape(a,b,HEADS,WZ,WZ,WLAT,WLAT,23)
    side=np.arange(WLAT)<WLAT//2
    split=jnp.asarray(side[:,None]!=side[None,:])[:,:,None]
    ai=jnp.arange(a).reshape(a,1,1,1,1,1,1,1); bi=jnp.arange(b).reshape(1,b,1,1,1,1,1,1)
    zq=jnp.arange(WZ).reshape(1,1,1,WZ,1,1,1,1); zk=jnp.arange(WZ).reshape(1,1,1,1,WZ,1,1,1)
    cut=(lat0&(ai==0)&split)|((bi==0)&(zq!=zk))
    t=jnp.where(cut,MASKED,t)
    t=t.transpose(0,1,2,3,4,6,7,5).reshape(a,b,HEADS,WZ,WZ,WLAT,138)
    v=jnp.stack([t[...,18-6*d:138-6*d] for d in range(4)],axis=5)
    v=jnp.pad(v,((0,0),)*7+((0,8),))
    return v.reshape(a,b,HEADS,WZ,WZ,24,128)

def unfold_grad(g):
    n=g.shape[0]
    v=jnp.concatenate([g[:,:6],g[:,6,:60].reshape(n,6,10)],axis=-1)
    return v.reshape(n,WLAT,23,WLAT).transpose(0,3,1,2).reshape(n,828)

LON = ("xl", "y", "z")
LAT = ("xh", "c")
ZWIN = 4
GRAD_SCALE = 1.0 / math.sqrt(294912)


def along(block, axis, distance):
    size = lax.axis_size(axis)
    return lax.ppermute(block, axis, [(i, (i + distance) % size) for i in range(size)])


def on_device(air_state, cotangent, norm_gain, norm_shift, qkv_weight, proj_weight, earth_bias):
    half = WLON // 2
    rows_up = WLAT // 2
    both = jnp.stack((air_state, cotangent))
    west = jnp.concatenate((both[:, 7:], both[:, :3]), axis=1)
    east = both[:, 3:7]
    from_west = along(west[..., half:, :], LON, 1)
    from_east = along(east[..., :half, :], LON, -1)
    west = jnp.concatenate((from_west, west[..., :half, :]), axis=3)
    east = jnp.concatenate((east[..., half:, :], from_east), axis=3)
    grid = jnp.concatenate((west, east), axis=1)
    below = along(grid[:, :, 2 * WLAT - rows_up :], LAT, 1)
    grid = jnp.concatenate((below, grid[:, :, : 2 * WLAT - rows_up]), axis=2)
    win = grid.reshape(2, ZWIN, WZ, 2, WLAT, WLON, C).transpose(0, 1, 3, 2, 5, 4, 6).reshape(2, ZWIN, 2, WTOK, C)

    lat = lax.axis_index(LAT)
    table = spread_table(earth_bias, lat == 0)
    out_win, grad_win, fold, wgrad = attend(win[0], win[1], norm_gain, norm_shift, qkv_weight, proj_weight, table)
    wgrad = wgrad.reshape(2, 64, 16, 128)[:, :, :11].astype(BF16)

    core = lax.axis_index("c")
    kept = lax.dynamic_index_in_dim(wgrad, core, 0, keepdims=False)
    other = along(lax.dynamic_index_in_dim(wgrad, 1 - core, 0, keepdims=False), "c", 1)
    wpart = (kept.astype(F32) + other.astype(F32)).astype(BF16)
    payload = jnp.concatenate((fold.reshape(64, 24, 128)[:, :21].astype(BF16), wpart), axis=1)
    parts = lax.all_to_all(payload, LON, 0, 0, tiled=True)
    mine = jnp.sum(parts.astype(F32), axis=0)
    wsum = mine[21:]
    wsum = (wsum + along(wsum, "xh", 1)) * GRAD_SCALE
    bsum = unfold_grad(mine[:21].reshape(3, 7, 128)).reshape(-1)
    bsum = jnp.pad(bsum, (0, 20 * 128 - bsum.shape[0])).reshape(20, 128)
    shard = jnp.concatenate((bsum, wsum), axis=0).astype(BF16)
    shard = jnp.pad(shard, ((0, 1), (0, 0)))
    spread = lax.all_to_all(jnp.broadcast_to(shard, (64,) + shard.shape), LON, 0, 0, tiled=True)
    bias_grad = spread[:, :20].reshape(64, 2560)[:, :2484].reshape(2, ZWIN, HEADS, POSITIONS)
    whalf = spread[:, 20:29]
    nhalf = wsum[9:11]
    wother = along(whalf, "c", 1)
    nother = along(nhalf, "c", 1)
    first = core == 0
    w0 = jnp.where(first, whalf, wother)
    w1 = jnp.where(first, wother, whalf)
    wall = jnp.concatenate((w0, w1), axis=1).reshape(C, 4 * C).astype(F32)
    gain_grad = jnp.where(first, nhalf, nother).reshape(256)[:C]
    shift_grad = jnp.where(first, nother, nhalf).reshape(256)[:C]

    outs = jnp.stack((out_win, grad_win))
    grid = outs.reshape(2, ZWIN, 2, WZ, WLON, WLAT, C).transpose(0, 1, 3, 2, 5, 4, 6).reshape(2, 2 * ZWIN, 2 * WLAT, WLON, C)
    above = along(grid[:, :, :rows_up], LAT, -1)
    grid = jnp.concatenate((grid[:, :, rows_up:], above), axis=2)
    west, east = grid[:, :4], grid[:, 4:]
    back_east = along(west[..., :half, :], LON, -1)
    back_west = along(east[..., half:, :], LON, 1)
    west = jnp.concatenate((west[..., half:, :], back_east), axis=3)
    east = jnp.concatenate((back_west, east[..., :half, :]), axis=3)
    both = jnp.concatenate((west[:, 1:], east, west[:, :1]), axis=1)
    return both[0], both[1], wall[:, : 3 * C], wall[:, 3 * C :], gain_grad, shift_grad, bias_grad


def solution(mesh):
    fine = Mesh(mesh.devices.reshape(2, 4, 8, 2, 2), LON + LAT)
    token = P(None, LAT, LON, None)
    table = P(LAT, None, None, None)
    return jax.shard_map(
        on_device,
        mesh=fine,
        in_specs=(token, token, P(), P(), P(), P(), table),
        out_specs=(token, token, P(), P(), P(), P(), table),
        check_vma=False,
    )
```

```python
import functools
import math

import jax
import jax.numpy as jnp
import numpy as np
from jax import lax
from jax.experimental import pallas as pl
from jax.experimental.pallas import tpu as pltpu
from jax.sharding import Mesh, PartitionSpec as P

HEADS=6; WZ=2; WLAT=6; WLON=12; WTOK=144; POSITIONS=3312
C=192; HD=32
EPSILON=1e-5
MASKED=-1e30
QP=896
GL=72
F32=jnp.float32; BF16=jnp.bfloat16
SCALE=HD**-0.5

def nn(a,b): return lax.dot_general(a,b,(((1,),(0,)),((),())),preferred_element_type=F32)
def nt(a,b): return lax.dot_general(a,b,(((1,),(1,)),((),())),preferred_element_type=F32)
def tn(a,b): return lax.dot_general(a,b,(((0,),(0,)),((),())),preferred_element_type=F32)

def tile_groups(t):
    out=[]
    for g in range(12):
        lo=max(GL*g-128*t,0); hi=min(GL*(g+1)-128*t,128)
        if lo<hi: out.append((g,lo,hi))
    return out

def window(w, b, x_scr,o_scr,gain,shift,wq,wk,wv,wkT,wvT,wp,bias_ref,
           fold_ref, s_scr,dp_scr,ph_scr,ds_scr,fold_scr, normed_scr,gq_scr,gk_scr,gv_scr,ctx_scr,up_scr,tail_scr,row7_scr,
           eye144, base):
    toks=pl.ds(pl.multiple_of(b*WTOK,WTOK),WTOK)
    x=x_scr[0,toks].astype(F32)
    u=x_scr[1,toks]
    mean=jnp.mean(x,axis=-1,keepdims=True)
    cen=x-mean
    inv=lax.rsqrt(jnp.mean(cen*cen,axis=-1,keepdims=True)+EPSILON)
    std=cen*inv
    normed=(std*gain+shift).astype(BF16)
    q=nn(normed,wq).astype(BF16)
    k=nn(normed,wk).astype(BF16)
    v=nn(normed,wv).astype(BF16)
    kT=nt(wkT,normed).astype(BF16)
    vT=nt(wvT,normed).astype(BF16)
    dctx=nt(u,wp).astype(BF16)
    lane_c=lax.broadcasted_iota(jnp.int32,(1,C),1)//HD
    def blocks(m):
        zero=jnp.zeros_like(m)
        parts=[jnp.where(lane_c==h,m,zero) for h in range(HEADS)]
        return jnp.concatenate(parts+[jnp.zeros((QP-HEADS*WTOK,C),BF16)],axis=0)
    qblk=blocks(q); dblk=blocks(dctx)
    s_scr[w]=nt(k,qblk)
    dp_scr[w]=nt(v,dblk)
    lane=lax.broadcasted_iota(jnp.int32,(24,128),1)
    acc={}
    for t in range(7):
        groups=tile_groups(t)
        rows=[]
        for zk in range(WZ):
            for j in range(3):
                tile=None
                for (g,lo,hi) in groups:
                    h,zq=g//2,g%2
                    shift_=(GL*g-128*t-24*(2-j))%128
                    piece=bias_ref[0,h,w,zq,zk]
                    if shift_: piece=pltpu.roll(piece,shift_,1)
                    tile=piece if tile is None else jnp.where(lane>=lo,piece,tile)
                if groups[-1][2]<128: tile=jnp.where(lane<groups[-1][2],tile,0.0)
                rows.append(tile)
        bias=jnp.concatenate(rows,axis=0)
        cols=slice(128*t,128*(t+1))
        s=s_scr[w,:,cols]*SCALE+bias
        m=jnp.max(s,axis=0,keepdims=True)
        e=jnp.exp(s-m)
        p=e*(1.0/jnp.sum(e,axis=0,keepdims=True))
        ph_scr[w,:,cols]=p.astype(BF16)
        dp=dp_scr[w,:,cols]
        ds=p*(dp-jnp.sum(p*dp,axis=0,keepdims=True))
        ds_scr[w,:,cols]=(ds*SCALE).astype(BF16)
        for zk in range(WZ):
            for (g,lo,hi) in groups:
                tot=None
                for j in range(3):
                    r0=zk*72+24*j
                    piece=ds[r0:r0+24]
                    if lo>0 or hi<128:
                        piece=jnp.where((lane>=lo)&(lane<hi),piece,0.0)
                    back=(-(GL*g-128*t-24*(2-j)))%128
                    if back: piece=pltpu.roll(piece,back,1)
                    tot=piece if tot is None else tot+piece
                h,zq=g//2,g%2
                if GL*g-128*t>=0:
                    fold_scr[w,h,zq,zk]=tot
                else:
                    fold_scr[w,h,zq,zk]+=tot
    for h in range(HEADS):
        for zq in range(WZ):
            for zk in range(WZ):
                f=fold_scr[w,h,zq,zk]
                lo_t=None; hi_t=None
                lane6=lax.broadcasted_iota(jnp.int32,(8,128),1)
                for dw in range(4):
                    part=jnp.concatenate([f[6*dw:6*dw+6],jnp.zeros((2,128),F32)],axis=0)
                    sh=18-6*dw
                    r=pltpu.roll(part,sh,1) if sh else part
                    a=jnp.where(lane6>=sh,r,0.0) if sh>8 else r
                    lo_t=a if lo_t is None else lo_t+a
                    if sh>8:
                        b=jnp.where(lane6<sh-8,r,0.0)
                        hi_t=b if hi_t is None else hi_t+b
                n=(h*WZ+zq)*WZ+zk
                fold_ref[0,w,24*(n//3)+7*(n%3):24*(n//3)+7*(n%3)+6]=lo_t[:6]
                tail_scr[w,8*n:8*n+8]=hi_t
    tail=tail_scr[w,pl.ds(0,24,stride=8),:]
    for hk in range(1,WLAT):
        tail=tail+pltpu.roll(tail_scr[w,pl.ds(hk,24,stride=8),:],10*hk,1)
    row7_scr[w]=tail
    for m in range(3):
        fold_ref[0,w,pl.ds(7*m+6,8,stride=24),:]=row7_scr[w,pl.ds(m,8,stride=3),:]
    ph=ph_scr[w]; dsc=ds_scr[w]
    ctxT=jnp.concatenate([nn(vT[32*h:32*h+32],ph[:,128*h:128*h+256])[:,16*h:16*h+WTOK] for h in range(HEADS)],axis=0).astype(BF16)
    dqT=jnp.concatenate([nn(kT[32*h:32*h+32],dsc[:,128*h:128*h+256])[:,16*h:16*h+WTOK] for h in range(HEADS)],axis=0).astype(BF16)
    ctx=nt(eye144,ctxT).astype(BF16)
    dq=nt(eye144,dqT).astype(BF16)
    dv=nn(ph,dblk).astype(BF16)
    dk=nn(dsc,qblk).astype(BF16)
    o_scr[0,toks]=(x+nn(ctx,wp)).astype(BF16)
    ng=nt(dq,wq)+nt(dk,wk)+nt(dv,wv)
    g=ng*gain
    br=inv*(g-jnp.mean(g,axis=-1,keepdims=True)-std*jnp.mean(g*std,axis=-1,keepdims=True))
    o_scr[1,toks]=(u.astype(F32)+br).astype(BF16)
    rows=pl.ds(base+w*WTOK,WTOK)
    normed_scr[rows]=normed; gq_scr[rows]=dq; gk_scr[rows]=dk; gv_scr[rows]=dv; ctx_scr[rows]=ctx; up_scr[rows]=u
    return jnp.sum(ng*std,axis=0,keepdims=True), jnp.sum(ng,axis=0,keepdims=True)

def kernel(tl_ref,tr_ref,bl_ref,br_ref,left_ref,right_ref,perm_ref,back_ref,
           gain_ref,shift_ref,wq_ref,wk_ref,wv_ref,wkT_ref,wvT_ref,wp_ref,bias_ref,
           otl_ref,otr_ref,obl_ref,obr_ref,oleft_ref,oright_ref,fold_ref,wgrad_ref,x_scr,o_scr,*scr):
    w_scr,ngrad_scr=scr[13:]
    a=pl.program_id(0); pair=pl.program_id(1)
    step=a*2+pair
    half=slice(0,WTOK); rest=slice(WTOK,2*WTOK)
    @pl.when((a==0)&(pair==0))
    def _():
        for s in range(2):
            t=jnp.concatenate([tl_ref[s],tr_ref[s],bl_ref[s],br_ref[s]],axis=0)
            x_scr[s]=nn(perm_ref[...],t).astype(BF16)
    @pl.when((a==1)&(pair==0))
    def _():
        for s in range(2):
            t=jnp.concatenate([left_ref[s,half],right_ref[s,half],left_ref[s,rest],right_ref[s,rest]],axis=0)
            x_scr[s]=nn(perm_ref[...],t).astype(BF16)
    eye=(lax.broadcasted_iota(jnp.int32,(WTOK,WTOK),0)==lax.broadcasted_iota(jnp.int32,(WTOK,WTOK),1)).astype(BF16)
    base=pl.multiple_of(step*2*WTOK,2*WTOK)
    gs=[]
    for w in range(2):
        gs.append(window(w,pair*2+w,x_scr,o_scr,gain_ref[...],shift_ref[...],wq_ref[...],wk_ref[...],wv_ref[...],wkT_ref[...],wvT_ref[...],wp_ref[...],bias_ref,
            fold_ref,*scr[:13],eye,base))
    @pl.when((a==0)&(pair==1))
    def _():
        for s in range(2):
            t=nn(back_ref[...],o_scr[s]).astype(BF16)
            for n,ref in enumerate((otl_ref,otr_ref,obl_ref,obr_ref)):
                ref[s]=t[WTOK*n:WTOK*(n+1)]
    @pl.when((a==1)&(pair==1))
    def _():
        for s in range(2):
            t=nn(back_ref[...],o_scr[s]).astype(BF16)
            oleft_ref[s,half]=t[:WTOK]; oright_ref[s,half]=t[WTOK:2*WTOK]
            oleft_ref[s,rest]=t[2*WTOK:3*WTOK]; oright_ref[s,rest]=t[3*WTOK:]
    both=jnp.concatenate([gs[0][0]+gs[1][0],gs[0][1]+gs[1][1],jnp.zeros((6,C),F32)],axis=0)
    @pl.when(step==0)
    def _(): ngrad_scr[...]=both
    @pl.when(step>0)
    def _(): ngrad_scr[...]+=both
    @pl.when(step==3)
    def _():
        normed_scr,gq_scr,gk_scr,gv_scr,ctx_scr,up_scr=scr[5:11]
        n=normed_scr[...]
        whole=jnp.concatenate([tn(n,gq_scr[...]),tn(n,gk_scr[...]),tn(n,gv_scr[...]),tn(ctx_scr[...],up_scr[...])],axis=1)
        for t in range(6):
            w_scr[C*t:C*(t+1)]=whole[:,128*t:128*(t+1)]
        for r in range(3):
            for t in range(6):
                m=r*6+t
                wgrad_ref[pl.ds((m//9)*64*16+m%9,64,stride=16),:]=w_scr[pl.ds(C*t+r,64,stride=3),:]
        ng=ngrad_scr[...]
        for half in range(2):
            wgrad_ref[pl.ds(half*64*16+9,64,stride=16),:]=jnp.broadcast_to(ng[half:half+1,:128],(64,128))
            wgrad_ref[pl.ds(half*64*16+10,64,stride=16),:]=jnp.broadcast_to(jnp.concatenate([ng[half:half+1,128:],jnp.zeros((1,64),F32)],axis=1),(64,128))

def token_order():
    hot=np.zeros((576,576),np.float32)
    for lev in range(8):
        for w in range(WLON):
            for h in range(WLAT):
                quad=h//3*2+w//6
                hot[(lev*WLON+w)*WLAT+h,quad*WTOK+h%3*48+w%6*8+(lev-1)%8]=1.0
    return hot

def attend(parts,gain,shift,wqkv,wp,vtab):
    wq,wk,wv=wqkv[:,:C],wqkv[:,C:2*C],wqkv[:,2*C:]
    full=lambda *s: pl.BlockSpec(s,lambda i,j:(0,)*len(s))
    tok=8*WTOK
    hot=token_order()
    grids=[full(*p.shape) for p in parts]
    return pl.pallas_call(
        kernel,
        grid=(2,2),
        in_specs=grids+[full(4*WTOK,4*WTOK)]*2+[full(1,C),full(1,C)]+[full(C,C)]*6+[pl.BlockSpec((1,HEADS,2,WZ,WZ,24,128),lambda i,j:(i,0,j,0,0,0,0))],
        out_specs=grids+[pl.BlockSpec((1,2,192,128),lambda i,j:(i,j,0,0)),full(2*64*16,128)],
        out_shape=[jax.ShapeDtypeStruct(p.shape,BF16) for p in parts]+[
                   jax.ShapeDtypeStruct((2,4,192,128),F32),
                   jax.ShapeDtypeStruct((2*64*16,128),F32)],
        scratch_shapes=[pltpu.VMEM((2,4*WTOK,C),BF16),pltpu.VMEM((2,4*WTOK,C),BF16),
                        pltpu.VMEM((2,WTOK,QP),F32),pltpu.VMEM((2,WTOK,QP),F32),pltpu.VMEM((2,WTOK,QP),BF16),pltpu.VMEM((2,WTOK,QP),BF16),
                        pltpu.VMEM((2,HEADS,WZ,WZ,24,128),F32)]+[pltpu.VMEM((tok,C),BF16)]*6
                       +[pltpu.VMEM((2,192,128),F32),pltpu.VMEM((2,24,128),F32)]+[pltpu.VMEM((6*C,128),F32),pltpu.VMEM((8,C),F32)],
        compiler_params=pltpu.CompilerParams(dimension_semantics=("arbitrary","arbitrary"),vmem_limit_bytes=32*1024*1024),
        cost_estimate=pl.CostEstimate(flops=6*10**9,bytes_accessed=8000000,transcendentals=10**6),
        name="attend",
    )(*parts,jnp.asarray(hot,BF16),jnp.asarray(hot.T,BF16),gain.reshape(1,C),shift.reshape(1,C),wq,wk,wv,wk.T,wv.T,wp,vtab)

def table_order():
    hot=np.zeros((828,896),np.float32)
    for hq in range(WLAT):
        for hk in range(WLAT):
            for o in range(23):
                i=o*WLAT+hq
                hot[(hq*WLAT+hk)*23+o,128*hk+i if i<128 else 768+10*hk+i-128]=1.0
    return hot

def table_kernel(lat_ref,t_ref,hot_ref,out_ref):
    rows=2*HEADS*4
    row=lax.broadcasted_iota(jnp.int32,(rows,128),0)
    lane=lax.broadcasted_iota(jnp.int32,(rows,128),1)
    low=lane%WLAT<WLAT//2
    edge=(row<rows//2)&(lat_ref[0]==0)
    bottom=row%4==0
    hot=hot_ref[...]
    for zz in range(4):
        t=t_ref[:,828*zz:828*(zz+1)]
        hi=t.astype(BF16); rest=t-hi.astype(F32)
        mid=rest.astype(BF16); lo=(rest-mid.astype(F32)).astype(BF16)
        v=nn(jnp.concatenate([hi,mid,lo],axis=0),hot)
        v=v[:rows]+v[rows:2*rows]+v[2*rows:]
        tail=v[:,768:896]
        for hk in range(WLAT):
            main=v[:,128*hk:128*(hk+1)]
            cut=edge&(low!=(hk<WLAT//2))
            if zz in (1,2): cut=cut|bottom
            for dw in range(4):
                s=18-6*dw
                r=pltpu.roll(main,128-s,1) if s else main
                if s>8:
                    r=jnp.where(lane>=128-s,pltpu.roll(tail,(128-s-10*hk)%128,1),r)
                out_ref[pl.ds(zz*24+dw*WLAT+hk,rows,stride=96),:]=jnp.where(cut,MASKED,r)

def spread_table(earth_bias, lat):
    flat=earth_bias.transpose(0,2,1,3).reshape(48,POSITIONS)
    whole=pl.BlockSpec(memory_space=pltpu.VMEM)
    out=pl.pallas_call(
        table_kernel,
        in_specs=[pl.BlockSpec(memory_space=pltpu.SMEM),whole,whole],
        out_specs=whole,
        out_shape=jax.ShapeDtypeStruct((48*96,128),F32),
        compiler_params=pltpu.CompilerParams(vmem_limit_bytes=16*1024*1024),
        cost_estimate=pl.CostEstimate(flops=2*576*828*896,bytes_accessed=5000000,transcendentals=0),
        name="table",
    )(jnp.full((1,),lat,jnp.int32),flat,jnp.asarray(table_order(),BF16))
    return out.reshape(2,HEADS,4,WZ,WZ,24,128)

def unfold_grad(g):
    n=g.shape[0]
    v=jnp.concatenate([g[:,:6],g[:,6,:60].reshape(n,6,10)],axis=-1)
    return v.reshape(n,WLAT,23,WLAT).transpose(0,3,1,2).reshape(n,828)

LON = ("xl", "y", "z")
LAT = ("xh", "c")
ZWIN = 4
GRAD_SCALE = 1.0 / math.sqrt(294912)


def along(block, axis, distance):
    size = lax.axis_size(axis)
    return lax.ppermute(block, axis, [(i, (i + distance) % size) for i in range(size)])


def across(block, lon_step, lat_step):
    lon, lat = lax.axis_size(LON), lax.axis_size(LAT)
    route = [
        (i * lat + j, (i + lon_step) % lon * lat + (j + lat_step) % lat)
        for i in range(lon)
        for j in range(lat)
    ]
    return lax.ppermute(block, LON + LAT, route)


def pack_kernel(x_ref, u_ref, *outs):
    west, east = slice(0, WLON // 2), slice(WLON // 2, WLON)
    upper, middle, lower = slice(0, WLAT // 2), slice(WLAT // 2, 3 * WLAT // 2), slice(3 * WLAT // 2, 2 * WLAT)
    places = ((middle, west), (upper, east), (lower, east), (lower, west), (upper, west), (middle, east))
    for ref, (rows, cols) in zip(outs, places):
        ref[0] = x_ref[rows, cols]
        ref[1] = u_ref[rows, cols]


def pack(x, u):
    whole = pl.BlockSpec(memory_space=pltpu.VMEM)
    half = WLON // 2
    shapes = [(2, rows, half, 8, C) for rows in (6, 3, 3, 3, 3, 6)]
    return pl.pallas_call(
        pack_kernel,
        in_specs=[whole, whole],
        out_specs=[whole] * 6,
        out_shape=[jax.ShapeDtypeStruct(s, BF16) for s in shapes],
        compiler_params=pltpu.CompilerParams(vmem_limit_bytes=8 * 1024 * 1024),
        name="pack",
    )(x, u)


def on_device(air_state, cotangent, norm_gain, norm_shift, qkv_weight, proj_weight, earth_bias):
    half = WLON // 2
    sent_right, sent_bottom, sent_corner, sent_above, own_upper, own_middle = [
        p.reshape(2, -1, C) for p in pack(air_state.transpose(1, 2, 0, 3), cotangent.transpose(1, 2, 0, 3))
    ]
    right = across(sent_right, -1, 0)
    bottom = across(sent_bottom, 1, 0)
    corner = across(sent_corner, 1, 1)
    above = across(sent_above, 0, 1)
    parts = [corner, above, bottom, own_upper, own_middle, right]
    table = spread_table(earth_bias, lax.axis_index(LAT))
    *outs, fold, wgrad = attend(parts, norm_gain, norm_shift, qkv_weight, proj_weight, table)
    wgrad = wgrad.reshape(2, 64, 16, 128)[:, :, :11].astype(BF16)

    corner, above, bottom, own_upper, own_middle, right = outs
    right = across(right, 1, 0)
    bottom = across(bottom, -1, 0)
    corner = across(corner, -1, -1)
    above = across(above, 0, -1)

    core = lax.axis_index("c")
    kept = lax.dynamic_index_in_dim(wgrad, core, 0, keepdims=False)
    other = along(lax.dynamic_index_in_dim(wgrad, 1 - core, 0, keepdims=False), "c", 1)
    wpart = (kept.astype(F32) + other.astype(F32)).astype(BF16)
    payload = jnp.concatenate((fold.reshape(64, 24, 128)[:, :21].astype(BF16), wpart), axis=1)
    parts = lax.all_to_all(payload, LON, 0, 0, tiled=True)
    mine = jnp.sum(parts.astype(F32), axis=0)
    wsum = mine[21:]
    wsum = (wsum + along(wsum, "xh", 1)) * GRAD_SCALE
    bsum = unfold_grad(mine[:21].reshape(3, 7, 128)).reshape(-1)
    bsum = jnp.pad(bsum, (0, 20 * 128 - bsum.shape[0])).reshape(20, 128)
    shard = jnp.concatenate((bsum, wsum), axis=0).astype(BF16)
    shard = jnp.pad(shard, ((0, 1), (0, 0)))
    shard, right, bottom, corner, above = lax.optimization_barrier((shard, right, bottom, corner, above))
    spread = lax.all_to_all(jnp.broadcast_to(shard, (64,) + shard.shape), LON, 0, 0, tiled=True)
    bias_grad = spread[:, :20].reshape(64, 2560)[:, :2484].reshape(2, ZWIN, HEADS, POSITIONS)
    whalf = spread[:, 20:29]
    nhalf = wsum[9:11]
    wother = along(whalf, "c", 1)
    nother = along(nhalf, "c", 1)
    first = core == 0
    w0 = jnp.where(first, whalf, wother)
    w1 = jnp.where(first, wother, whalf)
    wall = jnp.concatenate((w0, w1), axis=1).reshape(C, 4 * C).astype(F32)
    gain_grad = jnp.where(first, nhalf, nother).reshape(256)[:C]
    shift_grad = jnp.where(first, nother, nhalf).reshape(256)[:C]

    def joined(left, right):
        return jnp.concatenate([t.reshape(2, -1, half, 8, C) for t in (left, right)], axis=2)

    grid = jnp.concatenate((joined(own_upper, bottom), joined(right, own_middle), joined(above, corner)), axis=1)
    both = grid.transpose(0, 3, 1, 2, 4)

    return both[0], both[1], wall[:, : 3 * C], wall[:, 3 * C :], gain_grad, shift_grad, bias_grad


def solution(mesh):
    fine = Mesh(mesh.devices.reshape(2, 4, 8, 2, 2), LON + LAT)
    token = P(None, LAT, LON, None)
    table = P(LAT, None, None, None)
    return jax.shard_map(
        on_device,
        mesh=fine,
        in_specs=(token, token, P(), P(), P(), P(), table),
        out_specs=(token, token, P(), P(), P(), P(), table),
        check_vma=False,
    )
```

```python
import functools
import math

import jax
import jax.numpy as jnp
import numpy as np
from jax import lax
from jax.experimental import pallas as pl
from jax.experimental.pallas import tpu as pltpu
from jax.sharding import Mesh, PartitionSpec as P

HEADS=6; WZ=2; WLAT=6; WLON=12; WTOK=144; POSITIONS=3312
C=192; HD=32
EPSILON=1e-5
MASKED=-1e30
NW=4
QP=896
GL=72
F32=jnp.float32; BF16=jnp.bfloat16
SCALE=HD**-0.5

def nn(a,b): return lax.dot_general(a,b,(((1,),(0,)),((),())),preferred_element_type=F32)
def nt(a,b): return lax.dot_general(a,b,(((1,),(1,)),((),())),preferred_element_type=F32)
def tn(a,b): return lax.dot_general(a,b,(((0,),(0,)),((),())),preferred_element_type=F32)

def tile_groups(t):
    out=[]
    for g in range(12):
        lo=max(GL*g-128*t,0); hi=min(GL*(g+1)-128*t,128)
        if lo<hi: out.append((g,lo,hi))
    return out

def window(w, b, x_scr,o_scr,gain,shift,wq,wk,wv,wkT,wvT,wp,bias_ref,
           fold_ref, s_scr,dp_scr,ph_scr,ds_scr,fold_scr, normed_scr,gq_scr,gk_scr,gv_scr,ctx_scr,up_scr,tail_scr,row7_scr,
           eye144, base, result):
    toks=pl.ds(pl.multiple_of(b*WTOK,WTOK),WTOK)
    x=x_scr[0,toks].astype(F32)
    u=x_scr[1,toks]
    mean=jnp.mean(x,axis=-1,keepdims=True)
    cen=x-mean
    inv=lax.rsqrt(jnp.mean(cen*cen,axis=-1,keepdims=True)+EPSILON)
    std=cen*inv
    normed=(std*gain+shift).astype(BF16)
    q=nn(normed,wq).astype(BF16)
    k=nn(normed,wk).astype(BF16)
    v=nn(normed,wv).astype(BF16)
    kT=nt(wkT,normed).astype(BF16)
    vT=nt(wvT,normed).astype(BF16)
    dctx=nt(u,wp).astype(BF16)
    yield
    lane_c=lax.broadcasted_iota(jnp.int32,(1,C),1)//HD
    def blocks(m):
        zero=jnp.zeros_like(m)
        parts=[jnp.where(lane_c==h,m,zero) for h in range(HEADS)]
        return jnp.concatenate(parts+[jnp.zeros((QP-HEADS*WTOK,C),BF16)],axis=0)
    qblk=blocks(q); dblk=blocks(dctx)
    s_scr[w]=nt(k,qblk)
    dp_scr[w]=nt(v,dblk)
    yield
    lane=lax.broadcasted_iota(jnp.int32,(24,128),1)
    for t in range(7):
        yield
        groups=tile_groups(t)
        rows=[]
        for zk in range(WZ):
            for j in range(3):
                tile=None
                for (g,lo,hi) in groups:
                    h,zq=g//2,g%2
                    shift_=(GL*g-128*t-24*(2-j))%128
                    piece=bias_ref[0,h,w,zq,zk]
                    if shift_: piece=pltpu.roll(piece,shift_,1)
                    tile=piece if tile is None else jnp.where(lane>=lo,piece,tile)
                if groups[-1][2]<128: tile=jnp.where(lane<groups[-1][2],tile,0.0)
                rows.append(tile)
        bias=jnp.concatenate(rows,axis=0)
        cols=slice(128*t,128*(t+1))
        s=s_scr[w,:,cols]*SCALE+bias
        m=jnp.max(s,axis=0,keepdims=True)
        e=jnp.exp(s-m)
        p=e*(1.0/jnp.sum(e,axis=0,keepdims=True))
        ph_scr[w,:,cols]=p.astype(BF16)
        dp=dp_scr[w,:,cols]
        ds=p*(dp-jnp.sum(p*dp,axis=0,keepdims=True))
        ds_scr[w,:,cols]=(ds*SCALE).astype(BF16)
        for zk in range(WZ):
            for (g,lo,hi) in groups:
                tot=None
                for j in range(3):
                    r0=zk*72+24*j
                    piece=ds[r0:r0+24]
                    if lo>0 or hi<128:
                        piece=jnp.where((lane>=lo)&(lane<hi),piece,0.0)
                    back=(-(GL*g-128*t-24*(2-j)))%128
                    if back: piece=pltpu.roll(piece,back,1)
                    tot=piece if tot is None else tot+piece
                h,zq=g//2,g%2
                if GL*g-128*t>=0:
                    fold_scr[w,h,zq,zk]=tot
                else:
                    fold_scr[w,h,zq,zk]+=tot
    yield
    for h in range(HEADS):
        for zq in range(WZ):
            for zk in range(WZ):
                f=fold_scr[w,h,zq,zk]
                lo_t=None; hi_t=None
                lane6=lax.broadcasted_iota(jnp.int32,(8,128),1)
                for dw in range(4):
                    part=jnp.concatenate([f[6*dw:6*dw+6],jnp.zeros((2,128),F32)],axis=0)
                    sh=18-6*dw
                    r=pltpu.roll(part,sh,1) if sh else part
                    a=jnp.where(lane6>=sh,r,0.0) if sh>8 else r
                    lo_t=a if lo_t is None else lo_t+a
                    if sh>8:
                        b=jnp.where(lane6<sh-8,r,0.0)
                        hi_t=b if hi_t is None else hi_t+b
                n=(h*WZ+zq)*WZ+zk
                fold_ref[0,w,24*(n//3)+7*(n%3):24*(n//3)+7*(n%3)+6]=lo_t[:6]
                tail_scr[w,8*n:8*n+8]=hi_t
    tail=tail_scr[w,pl.ds(0,24,stride=8),:]
    for hk in range(1,WLAT):
        tail=tail+pltpu.roll(tail_scr[w,pl.ds(hk,24,stride=8),:],10*hk,1)
    row7_scr[w]=tail
    for m in range(3):
        fold_ref[0,w,pl.ds(7*m+6,8,stride=24),:]=row7_scr[w,pl.ds(m,8,stride=3),:]
    yield
    ph=ph_scr[w]; dsc=ds_scr[w]
    ctxT=jnp.concatenate([nn(vT[32*h:32*h+32],ph[:,128*h:128*h+256])[:,16*h:16*h+WTOK] for h in range(HEADS)],axis=0).astype(BF16)
    dqT=jnp.concatenate([nn(kT[32*h:32*h+32],dsc[:,128*h:128*h+256])[:,16*h:16*h+WTOK] for h in range(HEADS)],axis=0).astype(BF16)
    yield
    ctx=nt(eye144,ctxT).astype(BF16)
    dq=nt(eye144,dqT).astype(BF16)
    yield
    dv=nn(ph,dblk).astype(BF16)
    dk=nn(dsc,qblk).astype(BF16)
    o_scr[0,toks]=(x+nn(ctx,wp)).astype(BF16)
    yield
    ng=nt(dq,wq)+nt(dk,wk)+nt(dv,wv)
    g=ng*gain
    br=inv*(g-jnp.mean(g,axis=-1,keepdims=True)-std*jnp.mean(g*std,axis=-1,keepdims=True))
    o_scr[1,toks]=(u.astype(F32)+br).astype(BF16)
    rows=pl.ds(base+w*WTOK,WTOK)
    normed_scr[rows]=normed; gq_scr[rows]=dq; gk_scr[rows]=dk; gv_scr[rows]=dv; ctx_scr[rows]=ctx; up_scr[rows]=u
    result.append((jnp.sum(ng*std,axis=0,keepdims=True), jnp.sum(ng,axis=0,keepdims=True)))

def kernel(tl_ref,tr_ref,bl_ref,br_ref,left_ref,right_ref,perm_ref,back_ref,
           gain_ref,shift_ref,wq_ref,wk_ref,wv_ref,wkT_ref,wvT_ref,wp_ref,bias_ref,
           otl_ref,otr_ref,obl_ref,obr_ref,oleft_ref,oright_ref,fold_ref,wgrad_ref,x_scr,o_scr,*scr):
    w_scr,ngrad_scr=scr[13:]
    a=pl.program_id(0); pair=pl.program_id(1)
    step=a*(4//NW)+pair
    half=slice(0,WTOK); rest=slice(WTOK,2*WTOK)
    @pl.when((a==0)&(pair==0))
    def _():
        for s in range(2):
            t=jnp.concatenate([tl_ref[s],tr_ref[s],bl_ref[s],br_ref[s]],axis=0)
            x_scr[s]=nn(perm_ref[...],t).astype(BF16)
    @pl.when((a==1)&(pair==0))
    def _():
        for s in range(2):
            t=jnp.concatenate([left_ref[s,half],right_ref[s,half],left_ref[s,rest],right_ref[s,rest]],axis=0)
            x_scr[s]=nn(perm_ref[...],t).astype(BF16)
    eye=(lax.broadcasted_iota(jnp.int32,(WTOK,WTOK),0)==lax.broadcasted_iota(jnp.int32,(WTOK,WTOK),1)).astype(BF16)
    base=pl.multiple_of(step*NW*WTOK,NW*WTOK)
    gs=[]
    live=[window(w,pair*NW+w,x_scr,o_scr,gain_ref[...],shift_ref[...],wq_ref[...],wk_ref[...],wv_ref[...],wkT_ref[...],wvT_ref[...],wp_ref[...],bias_ref,
            fold_ref,*scr[:13],eye,base,gs) for w in range(NW)]
    done=object()
    while live:
        live=[g for g in live if next(g,done) is not done]
    @pl.when((a==0)&(pair==4//NW-1))
    def _():
        for s in range(2):
            t=nn(back_ref[...],o_scr[s]).astype(BF16)
            for n,ref in enumerate((otl_ref,otr_ref,obl_ref,obr_ref)):
                ref[s]=t[WTOK*n:WTOK*(n+1)]
    @pl.when((a==1)&(pair==4//NW-1))
    def _():
        for s in range(2):
            t=nn(back_ref[...],o_scr[s]).astype(BF16)
            oleft_ref[s,half]=t[:WTOK]; oright_ref[s,half]=t[WTOK:2*WTOK]
            oleft_ref[s,rest]=t[2*WTOK:3*WTOK]; oright_ref[s,rest]=t[3*WTOK:]
    both=jnp.concatenate([sum(g[0] for g in gs),sum(g[1] for g in gs),jnp.zeros((6,C),F32)],axis=0)
    @pl.when(step==0)
    def _(): ngrad_scr[...]=both
    @pl.when(step>0)
    def _(): ngrad_scr[...]+=both
    @pl.when(step==8//NW-1)
    def _():
        normed_scr,gq_scr,gk_scr,gv_scr,ctx_scr,up_scr=scr[5:11]
        n=normed_scr[...]
        whole=jnp.concatenate([tn(n,gq_scr[...]),tn(n,gk_scr[...]),tn(n,gv_scr[...]),tn(ctx_scr[...],up_scr[...])],axis=1)
        for t in range(6):
            w_scr[C*t:C*(t+1)]=whole[:,128*t:128*(t+1)]
        for r in range(3):
            for t in range(6):
                m=r*6+t
                wgrad_ref[pl.ds((m//9)*64*16+m%9,64,stride=16),:]=w_scr[pl.ds(C*t+r,64,stride=3),:]
        ng=ngrad_scr[...]
        for half in range(2):
            wgrad_ref[pl.ds(half*64*16+9,64,stride=16),:]=jnp.broadcast_to(ng[half:half+1,:128],(64,128))
            wgrad_ref[pl.ds(half*64*16+10,64,stride=16),:]=jnp.broadcast_to(jnp.concatenate([ng[half:half+1,128:],jnp.zeros((1,64),F32)],axis=1),(64,128))

def token_order():
    hot=np.zeros((576,576),np.float32)
    for lev in range(8):
        for w in range(WLON):
            for h in range(WLAT):
                quad=h//3*2+w//6
                hot[(lev*WLON+w)*WLAT+h,quad*WTOK+h%3*48+w%6*8+(lev-1)%8]=1.0
    return hot

def attend(parts,gain,shift,wqkv,wp,vtab):
    wq,wk,wv=wqkv[:,:C],wqkv[:,C:2*C],wqkv[:,2*C:]
    full=lambda *s: pl.BlockSpec(s,lambda i,j:(0,)*len(s))
    tok=8*WTOK
    hot=token_order()
    grids=[full(*p.shape) for p in parts]
    return pl.pallas_call(
        kernel,
        grid=(2,4//NW),
        in_specs=grids+[full(4*WTOK,4*WTOK)]*2+[full(1,C),full(1,C)]+[full(C,C)]*6+[pl.BlockSpec((1,HEADS,NW,WZ,WZ,24,128),lambda i,j:(i,0,j,0,0,0,0))],
        out_specs=grids+[pl.BlockSpec((1,NW,192,128),lambda i,j:(i,j,0,0)),full(2*64*16,128)],
        out_shape=[jax.ShapeDtypeStruct(p.shape,BF16) for p in parts]+[
                   jax.ShapeDtypeStruct((2,4,192,128),F32),
                   jax.ShapeDtypeStruct((2*64*16,128),F32)],
        scratch_shapes=[pltpu.VMEM((2,4*WTOK,C),BF16),pltpu.VMEM((2,4*WTOK,C),BF16),
                        pltpu.VMEM((NW,WTOK,QP),F32),pltpu.VMEM((NW,WTOK,QP),F32),pltpu.VMEM((NW,WTOK,QP),BF16),pltpu.VMEM((NW,WTOK,QP),BF16),
                        pltpu.VMEM((NW,HEADS,WZ,WZ,24,128),F32)]+[pltpu.VMEM((tok,C),BF16)]*6
                       +[pltpu.VMEM((NW,192,128),F32),pltpu.VMEM((NW,24,128),F32)]+[pltpu.VMEM((6*C,128),F32),pltpu.VMEM((8,C),F32)],
        compiler_params=pltpu.CompilerParams(dimension_semantics=("arbitrary","arbitrary"),vmem_limit_bytes=32*1024*1024),
        cost_estimate=pl.CostEstimate(flops=6*10**9,bytes_accessed=8000000,transcendentals=10**6),
        name="attend",
    )(*parts,jnp.asarray(hot,BF16),jnp.asarray(hot.T,BF16),gain.reshape(1,C),shift.reshape(1,C),wq,wk,wv,wk.T,wv.T,wp,vtab)

def table_order():
    hot=np.zeros((828,896),np.float32)
    for hq in range(WLAT):
        for hk in range(WLAT):
            for o in range(23):
                i=o*WLAT+hq
                hot[(hq*WLAT+hk)*23+o,128*hk+i if i<128 else 768+10*hk+i-128]=1.0
    return hot

def table_kernel(lat_ref,t_ref,hot_ref,out_ref):
    rows=2*HEADS*4
    row=lax.broadcasted_iota(jnp.int32,(rows,128),0)
    lane=lax.broadcasted_iota(jnp.int32,(rows,128),1)
    low=lane%WLAT<WLAT//2
    edge=(row<rows//2)&(lat_ref[0]==0)
    bottom=row%4==0
    hot=hot_ref[...]
    for zz in range(4):
        t=t_ref[:,828*zz:828*(zz+1)]
        hi=t.astype(BF16); rest=t-hi.astype(F32)
        mid=rest.astype(BF16); lo=(rest-mid.astype(F32)).astype(BF16)
        v=nn(jnp.concatenate([hi,mid,lo],axis=0),hot)
        v=v[:rows]+v[rows:2*rows]+v[2*rows:]
        tail=v[:,768:896]
        for hk in range(WLAT):
            main=v[:,128*hk:128*(hk+1)]
            cut=edge&(low!=(hk<WLAT//2))
            if zz in (1,2): cut=cut|bottom
            for dw in range(4):
                s=18-6*dw
                r=pltpu.roll(main,128-s,1) if s else main
                if s>8:
                    r=jnp.where(lane>=128-s,pltpu.roll(tail,(128-s-10*hk)%128,1),r)
                out_ref[pl.ds(zz*24+dw*WLAT+hk,rows,stride=96),:]=jnp.where(cut,MASKED,r)

def spread_table(earth_bias, lat):
    flat=earth_bias.transpose(0,2,1,3).reshape(48,POSITIONS)
    whole=pl.BlockSpec(memory_space=pltpu.VMEM)
    out=pl.pallas_call(
        table_kernel,
        in_specs=[pl.BlockSpec(memory_space=pltpu.SMEM),whole,whole],
        out_specs=whole,
        out_shape=jax.ShapeDtypeStruct((48*96,128),F32),
        compiler_params=pltpu.CompilerParams(vmem_limit_bytes=16*1024*1024),
        cost_estimate=pl.CostEstimate(flops=2*576*828*896,bytes_accessed=5000000,transcendentals=0),
        name="table",
    )(jnp.full((1,),lat,jnp.int32),flat,jnp.asarray(table_order(),BF16))
    return out.reshape(2,HEADS,4,WZ,WZ,24,128)

def unfold_grad(g):
    n=g.shape[0]
    v=jnp.concatenate([g[:,:6],g[:,6,:60].reshape(n,6,10)],axis=-1)
    return v.reshape(n,WLAT,23,WLAT).transpose(0,3,1,2).reshape(n,828)

LON = ("xl", "y", "z")
LAT = ("xh", "c")
ZWIN = 4
GRAD_SCALE = 1.0 / math.sqrt(294912)


def along(block, axis, distance):
    size = lax.axis_size(axis)
    return lax.ppermute(block, axis, [(i, (i + distance) % size) for i in range(size)])


def across(block, lon_step, lat_step):
    lon, lat = lax.axis_size(LON), lax.axis_size(LAT)
    route = [
        (i * lat + j, (i + lon_step) % lon * lat + (j + lat_step) % lat)
        for i in range(lon)
        for j in range(lat)
    ]
    return lax.ppermute(block, LON + LAT, route)


def pack_kernel(places, x_ref, u_ref, *refs):
    count = len(places)
    outs, held, sems = refs[:count], refs[count : 2 * count], refs[-1]
    arrive, leave = [], []
    for n, (rows, cols) in enumerate(places):
        for s, src in enumerate((x_ref, u_ref)):
            arrive.append(pltpu.make_async_copy(src.at[rows, cols], held[n].at[s], sems.at[0, n, s]))
            leave.append(pltpu.make_async_copy(held[n].at[s], outs[n].at[s], sems.at[1, n, s]))
    for copy in arrive:
        copy.start()
    for first, second in zip(arrive, leave):
        first.wait()
        second.start()
    for copy in leave:
        copy.wait()


def pack(x, u, places):
    shapes = [(2, rows.size, cols.size, 8, C) for rows, cols in places]
    outs = pl.pallas_call(
        functools.partial(pack_kernel, places),
        in_specs=[pl.BlockSpec(memory_space=pl.ANY)] * 2,
        out_specs=[pl.BlockSpec(memory_space=pl.ANY)] * len(places),
        out_shape=[jax.ShapeDtypeStruct(s, BF16) for s in shapes],
        scratch_shapes=[pltpu.VMEM(s, BF16) for s in shapes] + [pltpu.SemaphoreType.DMA((2, len(places), 2))],
        compiler_params=pltpu.CompilerParams(vmem_limit_bytes=60 * 1024 * 1024),
        name="pack",
    )(x, u)
    return [p.reshape(2, -1, C) for p in outs]


def on_device(air_state, cotangent, norm_gain, norm_shift, qkv_weight, proj_weight, earth_bias):
    half = WLON // 2
    west, east = pl.ds(0, half), pl.ds(half, half)
    upper, middle, lower = pl.ds(0, WLAT // 2), pl.ds(WLAT // 2, WLAT), pl.ds(3 * WLAT // 2, WLAT // 2)
    x, u = air_state.transpose(1, 2, 0, 3), cotangent.transpose(1, 2, 0, 3)
    sent_left, sent_corner, sent_above, sent_bottom = pack(
        x, u, ((middle, east), (lower, west), (lower, east), (upper, west))
    )
    left = across(sent_left, 1, 0)
    corner = across(sent_corner, -1, 1)
    above = across(sent_above, 0, 1)
    bottom = across(sent_bottom, -1, 0)
    own_upper, own_middle = pack(x, u, ((upper, east), (middle, west)))
    parts = [above, corner, own_upper, bottom, left, own_middle]
    table = spread_table(earth_bias, lax.axis_index(LAT))
    *outs, fold, wgrad = attend(parts, norm_gain, norm_shift, qkv_weight, proj_weight, table)
    wgrad = wgrad.reshape(2, 64, 16, 128)[:, :, :11].astype(BF16)

    above, corner, own_upper, bottom, left, own_middle = outs
    left = across(left, -1, 0)
    corner = across(corner, 1, -1)
    above = across(above, 0, -1)
    bottom = across(bottom, 1, 0)

    core = lax.axis_index("c")
    kept = lax.dynamic_index_in_dim(wgrad, core, 0, keepdims=False)
    other = along(lax.dynamic_index_in_dim(wgrad, 1 - core, 0, keepdims=False), "c", 1)
    wpart = (kept.astype(F32) + other.astype(F32)).astype(BF16)
    payload = jnp.concatenate((fold.reshape(64, 24, 128)[:, :21].astype(BF16), wpart), axis=1)
    parts = lax.all_to_all(payload, LON, 0, 0, tiled=True)
    mine = jnp.sum(parts.astype(F32), axis=0)
    wsum = mine[21:]
    wsum = (wsum + along(wsum, "xh", 1)) * GRAD_SCALE
    bsum = unfold_grad(mine[:21].reshape(3, 7, 128)).reshape(-1)
    bsum = jnp.pad(bsum, (0, 20 * 128 - bsum.shape[0])).reshape(20, 128)
    shard = jnp.concatenate((bsum, wsum), axis=0).astype(BF16)
    shard = jnp.pad(shard, ((0, 1), (0, 0)))
    shard, left, bottom, corner, above = lax.optimization_barrier((shard, left, bottom, corner, above))
    spread = lax.all_to_all(jnp.broadcast_to(shard, (64,) + shard.shape), LON, 0, 0, tiled=True)
    bias_grad = spread[:, :20].reshape(64, 2560)[:, :2484].reshape(2, ZWIN, HEADS, POSITIONS)
    whalf = spread[:, 20:29]
    nhalf = wsum[9:11]
    wother = along(whalf, "c", 1)
    nother = along(nhalf, "c", 1)
    first = core == 0
    w0 = jnp.where(first, whalf, wother)
    w1 = jnp.where(first, wother, whalf)
    wall = jnp.concatenate((w0, w1), axis=1).reshape(C, 4 * C).astype(F32)
    gain_grad = jnp.where(first, nhalf, nother).reshape(256)[:C]
    shift_grad = jnp.where(first, nother, nhalf).reshape(256)[:C]

    def joined(left, right):
        return jnp.concatenate([t.reshape(2, -1, half, 8, C) for t in (left, right)], axis=2)

    grid = jnp.concatenate((joined(bottom, own_upper), joined(own_middle, left), joined(corner, above)), axis=1)
    both = grid.transpose(0, 3, 1, 2, 4)

    return both[0], both[1], wall[:, : 3 * C], wall[:, 3 * C :], gain_grad, shift_grad, bias_grad


def solution(mesh):
    fine = Mesh(mesh.devices.reshape(2, 4, 8, 2, 2), LON + LAT)
    token = P(None, LAT, LON, None)
    table = P(LAT, None, None, None)
    return jax.shard_map(
        on_device,
        mesh=fine,
        in_specs=(token, token, P(), P(), P(), P(), table),
        out_specs=(token, token, P(), P(), P(), P(), table),
        check_vma=False,
    )
```

```python
import functools
import math

import jax
import jax.numpy as jnp
import numpy as np
from jax import lax
from jax.experimental import pallas as pl
from jax.experimental.pallas import tpu as pltpu
from jax.sharding import Mesh, PartitionSpec as P

HEADS=6; WZ=2; WLAT=6; WLON=12; WTOK=144; POSITIONS=3312
C=192; HD=32
EPSILON=1e-5
MASKED=-1e30
NW=4
QP=896
GL=72
F32=jnp.float32; BF16=jnp.bfloat16
SCALE=HD**-0.5

def nn(a,b): return lax.dot_general(a,b,(((1,),(0,)),((),())),preferred_element_type=F32)
def nt(a,b): return lax.dot_general(a,b,(((1,),(1,)),((),())),preferred_element_type=F32)
def tn(a,b): return lax.dot_general(a,b,(((0,),(0,)),((),())),preferred_element_type=F32)

def tile_groups(t):
    out=[]
    for g in range(12):
        lo=max(GL*g-128*t,0); hi=min(GL*(g+1)-128*t,128)
        if lo<hi: out.append((g,lo,hi))
    return out

def window(w, b, x_scr,o_scr,gain,shift,wq,wk,wv,wkT,wvT,wp,bias_ref,
           fold_ref, s_scr,dp_scr,ph_scr,ds_scr,fold_scr, normed_scr,gq_scr,gk_scr,gv_scr,ctx_scr,up_scr,tail_scr,row7_scr,
           eye144, base, result):
    toks=slice(b*WTOK,(b+1)*WTOK)
    x=x_scr[0,toks].astype(F32)
    u=x_scr[1,toks]
    mean=jnp.mean(x,axis=-1,keepdims=True)
    cen=x-mean
    inv=lax.rsqrt(jnp.mean(cen*cen,axis=-1,keepdims=True)+EPSILON)
    std=cen*inv
    normed=(std*gain+shift).astype(BF16)
    q=nn(normed,wq).astype(BF16)
    k=nn(normed,wk).astype(BF16)
    v=nn(normed,wv).astype(BF16)
    kT=nt(wkT,normed).astype(BF16)
    vT=nt(wvT,normed).astype(BF16)
    dctx=nt(u,wp).astype(BF16)
    yield
    lane_c=lax.broadcasted_iota(jnp.int32,(1,C),1)//HD
    def blocks(m):
        zero=jnp.zeros_like(m)
        parts=[jnp.where(lane_c==h,m,zero) for h in range(HEADS)]
        return jnp.concatenate(parts+[jnp.zeros((QP-HEADS*WTOK,C),BF16)],axis=0)
    qblk=blocks(q); dblk=blocks(dctx)
    s_scr[w]=nt(k,qblk)
    dp_scr[w]=nt(v,dblk)
    yield
    lane=lax.broadcasted_iota(jnp.int32,(24,128),1)
    for t in range(7):
        yield
        groups=tile_groups(t)
        rows=[]
        for zk in range(WZ):
            for j in range(3):
                tile=None
                for (g,lo,hi) in groups:
                    h,zq=g//2,g%2
                    shift_=(GL*g-128*t-24*(2-j))%128
                    piece=bias_ref[0,h,w,zq,zk]
                    if shift_: piece=pltpu.roll(piece,shift_,1)
                    tile=piece if tile is None else jnp.where(lane>=lo,piece,tile)
                if groups[-1][2]<128: tile=jnp.where(lane<groups[-1][2],tile,0.0)
                rows.append(tile)
        bias=jnp.concatenate(rows,axis=0)
        cols=slice(128*t,128*(t+1))
        s=s_scr[w,:,cols]*SCALE+bias
        m=jnp.max(s,axis=0,keepdims=True)
        e=jnp.exp(s-m)
        p=e*(1.0/jnp.sum(e,axis=0,keepdims=True))
        ph_scr[w,:,cols]=p.astype(BF16)
        dp=dp_scr[w,:,cols]
        ds=p*(dp-jnp.sum(p*dp,axis=0,keepdims=True))
        ds_scr[w,:,cols]=(ds*SCALE).astype(BF16)
        for zk in range(WZ):
            for (g,lo,hi) in groups:
                tot=None
                for j in range(3):
                    r0=zk*72+24*j
                    piece=ds[r0:r0+24]
                    if lo>0 or hi<128:
                        piece=jnp.where((lane>=lo)&(lane<hi),piece,0.0)
                    back=(-(GL*g-128*t-24*(2-j)))%128
                    if back: piece=pltpu.roll(piece,back,1)
                    tot=piece if tot is None else tot+piece
                h,zq=g//2,g%2
                if GL*g-128*t>=0:
                    fold_scr[w,h,zq,zk]=tot
                else:
                    fold_scr[w,h,zq,zk]+=tot
    yield
    for h in range(HEADS):
        for zq in range(WZ):
            for zk in range(WZ):
                f=fold_scr[w,h,zq,zk]
                lo_t=None; hi_t=None
                lane6=lax.broadcasted_iota(jnp.int32,(8,128),1)
                for dw in range(4):
                    part=jnp.concatenate([f[6*dw:6*dw+6],jnp.zeros((2,128),F32)],axis=0)
                    sh=18-6*dw
                    r=pltpu.roll(part,sh,1) if sh else part
                    a=jnp.where(lane6>=sh,r,0.0) if sh>8 else r
                    lo_t=a if lo_t is None else lo_t+a
                    if sh>8:
                        b=jnp.where(lane6<sh-8,r,0.0)
                        hi_t=b if hi_t is None else hi_t+b
                n=(h*WZ+zq)*WZ+zk
                fold_ref[0,w,24*(n//3)+7*(n%3):24*(n//3)+7*(n%3)+6]=lo_t[:6]
                tail_scr[w,8*n:8*n+8]=hi_t
    tail=tail_scr[w,pl.ds(0,24,stride=8),:]
    for hk in range(1,WLAT):
        tail=tail+pltpu.roll(tail_scr[w,pl.ds(hk,24,stride=8),:],10*hk,1)
    row7_scr[w]=tail
    for m in range(3):
        fold_ref[0,w,pl.ds(7*m+6,8,stride=24),:]=row7_scr[w,pl.ds(m,8,stride=3),:]
    yield
    ph=ph_scr[w]; dsc=ds_scr[w]
    ctxT=jnp.concatenate([nn(vT[32*h:32*h+32],ph[:,128*h:128*h+256])[:,16*h:16*h+WTOK] for h in range(HEADS)],axis=0).astype(BF16)
    dqT=jnp.concatenate([nn(kT[32*h:32*h+32],dsc[:,128*h:128*h+256])[:,16*h:16*h+WTOK] for h in range(HEADS)],axis=0).astype(BF16)
    yield
    ctx=nt(eye144,ctxT).astype(BF16)
    dq=nt(eye144,dqT).astype(BF16)
    yield
    dv=nn(ph,dblk).astype(BF16)
    dk=nn(dsc,qblk).astype(BF16)
    o_scr[0,toks]=(x+nn(ctx,wp)).astype(BF16)
    yield
    ng=nt(dq,wq)+nt(dk,wk)+nt(dv,wv)
    g=ng*gain
    br=inv*(g-jnp.mean(g,axis=-1,keepdims=True)-std*jnp.mean(g*std,axis=-1,keepdims=True))
    o_scr[1,toks]=(u.astype(F32)+br).astype(BF16)
    rows=slice(base+w*WTOK,base+(w+1)*WTOK)
    normed_scr[rows]=normed; gq_scr[rows]=dq; gk_scr[rows]=dk; gv_scr[rows]=dv; ctx_scr[rows]=ctx; up_scr[rows]=u
    result.append((jnp.sum(ng*std,axis=0,keepdims=True), jnp.sum(ng,axis=0,keepdims=True)))

def kernel(first, *refs):
    count=2 if first else 4
    ins=refs[:count]
    perm_ref,back_ref,gain_ref,shift_ref,wqkv_ref,wp_ref,bias_ref=refs[count:count+7]
    refs=refs[count+7:]
    if first:
        outs,refs=refs[:2],refs[2:]
        fold_ref,w_ref,ngrad_ref,x_scr,o_scr=refs[:5]
    else:
        w_in,ngrad_in=refs[:2]
        outs,refs=refs[2:6],refs[6:]
        fold_ref,wgrad_ref,x_scr,o_scr,w_ref=refs[:5]
    scr=refs[5:]
    half=slice(0,WTOK); rest=slice(WTOK,2*WTOK)
    for s in range(2):
        if first:
            t=[ins[0][s,half],ins[1][s,half],ins[0][s,rest],ins[1][s,rest]]
        else:
            t=[ref[s] for ref in ins]
        x_scr[s]=nn(perm_ref[...],jnp.concatenate(t,axis=0)).astype(BF16)
    eye=(lax.broadcasted_iota(jnp.int32,(WTOK,WTOK),0)==lax.broadcasted_iota(jnp.int32,(WTOK,WTOK),1)).astype(BF16)
    wqkv=wqkv_ref[...]
    wq,wk,wv=wqkv[:,:C],wqkv[:,C:2*C],wqkv[:,2*C:]
    flip=(lax.broadcasted_iota(jnp.int32,(C,C),0)==lax.broadcasted_iota(jnp.int32,(C,C),1)).astype(BF16)
    wkT,wvT=nt(flip,wk).astype(BF16),nt(flip,wv).astype(BF16)
    gs=[]
    live=[window(w,w,x_scr,o_scr,gain_ref[...],shift_ref[...],wq,wk,wv,wkT,wvT,wp_ref[...],bias_ref,
            fold_ref,*scr,eye,0,gs) for w in range(NW)]
    done=object()
    while live:
        live=[g for g in live if next(g,done) is not done]
    for s in range(2):
        t=nn(back_ref[...],o_scr[s]).astype(BF16)
        if first:
            outs[0][s,half]=t[:WTOK]; outs[1][s,half]=t[WTOK:2*WTOK]
            outs[0][s,rest]=t[2*WTOK:3*WTOK]; outs[1][s,rest]=t[3*WTOK:]
        else:
            for n,ref in enumerate(outs):
                ref[s]=t[WTOK*n:WTOK*(n+1)]
    normed_scr,gq_scr,gk_scr,gv_scr,ctx_scr,up_scr=scr[5:11]
    n=normed_scr[...]
    whole=jnp.concatenate([tn(n,gq_scr[...]),tn(n,gk_scr[...]),tn(n,gv_scr[...]),tn(ctx_scr[...],up_scr[...])],axis=1)
    ng=jnp.concatenate([sum(g[0] for g in gs),sum(g[1] for g in gs),jnp.zeros((6,C),F32)],axis=0)
    if first:
        for t in range(6):
            w_ref[C*t:C*(t+1)]=whole[:,128*t:128*(t+1)]
        ngrad_ref[...]=ng
        return
    for t in range(6):
        w_ref[C*t:C*(t+1)]=whole[:,128*t:128*(t+1)]+w_in[C*t:C*(t+1)]
    ng=ng+ngrad_in[...]
    for r in range(3):
        for t in range(6):
            m=r*6+t
            wgrad_ref[pl.ds((m//9)*64*16+m%9,64,stride=16),:]=w_ref[pl.ds(C*t+r,64,stride=3),:]
    for h in range(2):
        wgrad_ref[pl.ds(h*64*16+9,64,stride=16),:]=jnp.broadcast_to(ng[h:h+1,:128],(64,128))
        wgrad_ref[pl.ds(h*64*16+10,64,stride=16),:]=jnp.broadcast_to(jnp.concatenate([ng[h:h+1,128:],jnp.zeros((1,64),F32)],axis=1),(64,128))

def token_order():
    hot=np.zeros((576,576),np.float32)
    for lev in range(8):
        for w in range(WLON):
            for h in range(WLAT):
                quad=h//3*2+w//6
                hot[(lev*WLON+w)*WLAT+h,quad*WTOK+h%3*48+w%6*8+(lev-1)%8]=1.0
    return hot

def attend(row,parts,weights,vtab,sums=()):
    first=row==1
    full=lambda *s: pl.BlockSpec(s,lambda i:(0,)*len(s))
    tok=4*WTOK
    hot=token_order()
    own=[full(*p.shape) for p in parts]
    wsum=pltpu.VMEM((6*C,128),F32)
    ends=[(6*C,128),(8,C)] if first else [(2*64*16,128)]
    return pl.pallas_call(
        functools.partial(kernel,first),
        grid=(1,),
        in_specs=own+[full(tok,tok)]*2+[full(1,C),full(1,C),full(C,3*C),full(C,C)]
                 +[pl.BlockSpec((1,HEADS,4,WZ,WZ,24,128),lambda i:(row,0,0,0,0,0,0))]+[full(*s.shape) for s in sums],
        out_specs=own+[full(1,4,192,128)]+[full(*s) for s in ends],
        out_shape=[jax.ShapeDtypeStruct(p.shape,BF16) for p in parts]+[jax.ShapeDtypeStruct((1,4,192,128),F32)]
                  +[jax.ShapeDtypeStruct(s,F32) for s in ends],
        scratch_shapes=[pltpu.VMEM((2,tok,C),BF16),pltpu.VMEM((2,tok,C),BF16)]+([] if first else [wsum])
                       +[pltpu.VMEM((NW,WTOK,QP),F32),pltpu.VMEM((NW,WTOK,QP),F32),pltpu.VMEM((NW,WTOK,QP),BF16),pltpu.VMEM((NW,WTOK,QP),BF16),
                        pltpu.VMEM((NW,HEADS,WZ,WZ,24,128),F32)]+[pltpu.VMEM((tok,C),BF16)]*6
                       +[pltpu.VMEM((NW,192,128),F32),pltpu.VMEM((NW,24,128),F32)],
        compiler_params=pltpu.CompilerParams(dimension_semantics=("arbitrary",),vmem_limit_bytes=32*1024*1024),
        cost_estimate=pl.CostEstimate(flops=3*10**9,bytes_accessed=4000000,transcendentals=5*10**5),
        name="attend_first" if first else "attend_last",
    )(*parts,jnp.asarray(hot,BF16),jnp.asarray(hot.T,BF16),*weights,vtab,*sums)

def table_order():
    hot=np.zeros((828,896),np.float32)
    for hq in range(WLAT):
        for hk in range(WLAT):
            for o in range(23):
                i=o*WLAT+hq
                hot[(hq*WLAT+hk)*23+o,128*hk+i if i<128 else 768+10*hk+i-128]=1.0
    return hot

def table_kernel(lat_ref,t_ref,hot_ref,out_ref):
    rows=2*HEADS*4
    row=lax.broadcasted_iota(jnp.int32,(rows,128),0)
    lane=lax.broadcasted_iota(jnp.int32,(rows,128),1)
    low=lane%WLAT<WLAT//2
    edge=(row<rows//2)&(lat_ref[0]==0)
    bottom=row%4==0
    hot=hot_ref[...]
    for zz in range(4):
        t=jnp.concatenate([t_ref[a,h,:,828*zz:828*(zz+1)] for a in range(2) for h in range(HEADS)],axis=0)
        hi=t.astype(BF16); rest=t-hi.astype(F32)
        mid=rest.astype(BF16); lo=(rest-mid.astype(F32)).astype(BF16)
        v=nn(jnp.concatenate([hi,mid,lo],axis=0),hot)
        v=v[:rows]+v[rows:2*rows]+v[2*rows:]
        tail=v[:,768:896]
        for hk in range(WLAT):
            main=v[:,128*hk:128*(hk+1)]
            cut=edge&(low!=(hk<WLAT//2))
            if zz in (1,2): cut=cut|bottom
            for dw in range(4):
                s=18-6*dw
                r=pltpu.roll(main,128-s,1) if s else main
                if s>8:
                    r=jnp.where(lane>=128-s,pltpu.roll(tail,(128-s-10*hk)%128,1),r)
                out_ref[pl.ds(zz*24+dw*WLAT+hk,rows,stride=96),:]=jnp.where(cut,MASKED,r)

def spread_table(earth_bias, lat):
    flat=earth_bias.transpose(0,2,1,3)
    whole=pl.BlockSpec(memory_space=pltpu.VMEM)
    out=pl.pallas_call(
        table_kernel,
        in_specs=[pl.BlockSpec(memory_space=pltpu.SMEM),whole,whole],
        out_specs=whole,
        out_shape=jax.ShapeDtypeStruct((48*96,128),F32),
        compiler_params=pltpu.CompilerParams(vmem_limit_bytes=16*1024*1024),
        cost_estimate=pl.CostEstimate(flops=2*576*828*896,bytes_accessed=5000000,transcendentals=0),
        name="table",
    )(jnp.full((1,),lat,jnp.int32),flat,jnp.asarray(table_order(),BF16))
    return out.reshape(2,HEADS,4,WZ,WZ,24,128)

def unfold_grad(g):
    n=g.shape[0]
    v=jnp.concatenate([g[:,:6],g[:,6,:60].reshape(n,6,10)],axis=-1)
    return v.reshape(n,WLAT,23,WLAT).transpose(0,3,1,2).reshape(n,828)

LON = ("xl", "y", "z")
LAT = ("xh", "c")
ZWIN = 4
GRAD_SCALE = 1.0 / math.sqrt(294912)


def along(block, axis, distance):
    size = lax.axis_size(axis)
    return lax.ppermute(block, axis, [(i, (i + distance) % size) for i in range(size)])


def across(block, lon_step, lat_step):
    lon, lat = lax.axis_size(LON), lax.axis_size(LAT)
    route = [
        (i * lat + j, (i + lon_step) % lon * lat + (j + lat_step) % lat)
        for i in range(lon)
        for j in range(lat)
    ]
    return lax.ppermute(block, LON + LAT, route)


def pack_kernel(places, x_ref, u_ref, *refs):
    count = len(places)
    outs, held, sems = refs[:count], refs[count : 2 * count], refs[-1]
    arrive, leave = [], []
    for n, (rows, cols) in enumerate(places):
        for s, src in enumerate((x_ref, u_ref)):
            arrive.append(pltpu.make_async_copy(src.at[rows, cols], held[n].at[s], sems.at[0, n, s]))
            leave.append(pltpu.make_async_copy(held[n].at[s], outs[n].at[s], sems.at[1, n, s]))
    for copy in arrive:
        copy.start()
    for first, second in zip(arrive, leave):
        first.wait()
        second.start()
    for copy in leave:
        copy.wait()


def pack(x, u, places):
    shapes = [(2, rows.size, cols.size, 8, C) for rows, cols in places]
    outs = pl.pallas_call(
        functools.partial(pack_kernel, places),
        in_specs=[pl.BlockSpec(memory_space=pl.ANY)] * 2,
        out_specs=[pl.BlockSpec(memory_space=pl.ANY)] * len(places),
        out_shape=[jax.ShapeDtypeStruct(s, BF16) for s in shapes],
        scratch_shapes=[pltpu.VMEM(s, BF16) for s in shapes] + [pltpu.SemaphoreType.DMA((2, len(places), 2))],
        compiler_params=pltpu.CompilerParams(vmem_limit_bytes=60 * 1024 * 1024),
        name="pack",
    )(x, u)
    return [p.reshape(2, -1, C) for p in outs]


def on_device(air_state, cotangent, norm_gain, norm_shift, qkv_weight, proj_weight, earth_bias):
    half = WLON // 2
    west, east = pl.ds(0, half), pl.ds(half, half)
    upper, middle, lower = pl.ds(0, WLAT // 2), pl.ds(WLAT // 2, WLAT), pl.ds(3 * WLAT // 2, WLAT // 2)
    x, u = air_state.transpose(1, 2, 0, 3), cotangent.transpose(1, 2, 0, 3)
    sent_left, sent_corner, sent_above, sent_bottom, own_upper, own_middle = pack(
        x, u, ((middle, east), (lower, west), (lower, east), (upper, west), (upper, east), (middle, west))
    )
    left = across(sent_left, 1, 0)
    corner = across(sent_corner, -1, 1)
    above = across(sent_above, 0, 1)
    bottom = across(sent_bottom, -1, 0)
    table = spread_table(earth_bias, lax.axis_index(LAT))
    weights = (norm_gain.reshape(1, C), norm_shift.reshape(1, C), qkv_weight, proj_weight)
    left, own_middle, fold_first, *sums = attend(1, [left, own_middle], weights, table)
    left = across(left, -1, 0)
    above, corner, own_upper, bottom, fold_last, wgrad = attend(0, [above, corner, own_upper, bottom], weights, table, sums)
    fold = jnp.concatenate((fold_last, fold_first))
    wgrad = wgrad.reshape(2, 64, 16, 128)[:, :, :11].astype(BF16)

    corner = across(corner, 1, -1)
    above = across(above, 0, -1)
    bottom = across(bottom, 1, 0)

    core = lax.axis_index("c")
    kept = lax.dynamic_index_in_dim(wgrad, core, 0, keepdims=False)
    other = along(lax.dynamic_index_in_dim(wgrad, 1 - core, 0, keepdims=False), "c", 1)
    wpart = (kept.astype(F32) + other.astype(F32)).astype(BF16)
    payload = jnp.concatenate((fold.reshape(64, 24, 128)[:, :21].astype(BF16), wpart), axis=1)
    parts = lax.all_to_all(payload, LON, 0, 0, tiled=True)
    mine = jnp.sum(parts.astype(F32), axis=0)
    wsum = mine[21:]
    wsum = (wsum + along(wsum, "xh", 1)) * GRAD_SCALE
    bsum = unfold_grad(mine[:21].reshape(3, 7, 128)).reshape(-1)
    bsum = jnp.pad(bsum, (0, 20 * 128 - bsum.shape[0])).reshape(20, 128)
    shard = jnp.concatenate((bsum, wsum), axis=0).astype(BF16)
    shard = jnp.pad(shard, ((0, 1), (0, 0)))
    shard, left, bottom, corner, above = lax.optimization_barrier((shard, left, bottom, corner, above))
    spread = lax.all_to_all(jnp.broadcast_to(shard, (64,) + shard.shape), LON, 0, 0, tiled=True)
    bias_grad = spread[:, :20].reshape(64, 2560)[:, :2484].reshape(2, ZWIN, HEADS, POSITIONS)
    whalf = spread[:, 20:29]
    nhalf = wsum[9:11]
    wother = along(whalf, "c", 1)
    nother = along(nhalf, "c", 1)
    first = core == 0
    w0 = jnp.where(first, whalf, wother)
    w1 = jnp.where(first, wother, whalf)
    wall = jnp.concatenate((w0, w1), axis=1).reshape(C, 4 * C).astype(F32)
    gain_grad = jnp.where(first, nhalf, nother).reshape(256)[:C]
    shift_grad = jnp.where(first, nother, nhalf).reshape(256)[:C]

    def joined(left, right):
        return jnp.concatenate([t.reshape(2, -1, half, 8, C) for t in (left, right)], axis=2)

    grid = jnp.concatenate((joined(bottom, own_upper), joined(own_middle, left), joined(corner, above)), axis=1)
    both = grid.transpose(0, 3, 1, 2, 4)

    return both[0], both[1], wall[:, : 3 * C], wall[:, 3 * C :], gain_grad, shift_grad, bias_grad


def solution(mesh):
    fine = Mesh(mesh.devices.reshape(2, 4, 8, 2, 2), LON + LAT)
    token = P(None, LAT, LON, None)
    table = P(LAT, None, None, None)
    return jax.shard_map(
        on_device,
        mesh=fine,
        in_specs=(token, token, P(), P(), P(), P(), table),
        out_specs=(token, token, P(), P(), P(), P(), table),
        check_vma=False,
    )
```

```python
import functools
import math

import jax
import jax.numpy as jnp
import numpy as np
from jax import lax
from jax.experimental import pallas as pl
from jax.experimental.pallas import tpu as pltpu
from jax.sharding import Mesh, PartitionSpec as P

HEADS=6; WZ=2; WLAT=6; WLON=12; WTOK=144; POSITIONS=3312
C=192; HD=32
EPSILON=1e-5
MASKED=-1e30
NW=4
QP=896
GL=72
F32=jnp.float32; BF16=jnp.bfloat16
SCALE=HD**-0.5

def nn(a,b): return lax.dot_general(a,b,(((1,),(0,)),((),())),preferred_element_type=F32)
def nt(a,b): return lax.dot_general(a,b,(((1,),(1,)),((),())),preferred_element_type=F32)
def tn(a,b): return lax.dot_general(a,b,(((0,),(0,)),((),())),preferred_element_type=F32)

def tile_groups(t):
    out=[]
    for g in range(12):
        lo=max(GL*g-128*t,0); hi=min(GL*(g+1)-128*t,128)
        if lo<hi: out.append((g,lo,hi))
    return out

def window(w, b, x_scr,o_scr,gain,shift,wq,wk,wv,wkT,wvT,wp,bias_ref,
           fold_ref, s_scr,dp_scr,ph_scr,ds_scr,fold_scr, normed_scr,gq_scr,gk_scr,gv_scr,ctx_scr,up_scr,tail_scr,row7_scr,
           eye144, base, result):
    toks=slice(b*WTOK,(b+1)*WTOK)
    x=x_scr[0,toks].astype(F32)
    u=x_scr[1,toks]
    mean=jnp.mean(x,axis=-1,keepdims=True)
    cen=x-mean
    inv=lax.rsqrt(jnp.mean(cen*cen,axis=-1,keepdims=True)+EPSILON)
    std=cen*inv
    normed=(std*gain+shift).astype(BF16)
    q=nn(normed,wq).astype(BF16)
    k=nn(normed,wk).astype(BF16)
    v=nn(normed,wv).astype(BF16)
    kT=nt(wkT,normed).astype(BF16)
    vT=nt(wvT,normed).astype(BF16)
    dctx=nt(u,wp).astype(BF16)
    yield
    lane_c=lax.broadcasted_iota(jnp.int32,(1,C),1)//HD
    def blocks(m):
        zero=jnp.zeros_like(m)
        parts=[jnp.where(lane_c==h,m,zero) for h in range(HEADS)]
        return jnp.concatenate(parts+[jnp.zeros((QP-HEADS*WTOK,C),BF16)],axis=0)
    qblk=blocks(q); dblk=blocks(dctx)
    s_scr[w]=nt(k,qblk)
    dp_scr[w]=nt(v,dblk)
    yield
    lane=lax.broadcasted_iota(jnp.int32,(24,128),1)
    for t in range(7):
        yield
        groups=tile_groups(t)
        rows=[]
        for zk in range(WZ):
            for j in range(3):
                tile=None
                for (g,lo,hi) in groups:
                    h,zq=g//2,g%2
                    shift_=(GL*g-128*t-24*(2-j))%128
                    piece=bias_ref[0,h,w,zq,zk]
                    if shift_: piece=pltpu.roll(piece,shift_,1)
                    tile=piece if tile is None else jnp.where(lane>=lo,piece,tile)
                if groups[-1][2]<128: tile=jnp.where(lane<groups[-1][2],tile,0.0)
                rows.append(tile)
        bias=jnp.concatenate(rows,axis=0)
        cols=slice(128*t,128*(t+1))
        s=s_scr[w,:,cols]*SCALE+bias
        m=jnp.max(s,axis=0,keepdims=True)
        e=jnp.exp(s-m)
        p=e*(1.0/jnp.sum(e,axis=0,keepdims=True))
        ph_scr[w,:,cols]=p.astype(BF16)
        dp=dp_scr[w,:,cols]
        ds=p*(dp-jnp.sum(p*dp,axis=0,keepdims=True))
        ds_scr[w,:,cols]=(ds*SCALE).astype(BF16)
        for zk in range(WZ):
            for (g,lo,hi) in groups:
                tot=None
                for j in range(3):
                    r0=zk*72+24*j
                    piece=ds[r0:r0+24]
                    if lo>0 or hi<128:
                        piece=jnp.where((lane>=lo)&(lane<hi),piece,0.0)
                    back=(-(GL*g-128*t-24*(2-j)))%128
                    if back: piece=pltpu.roll(piece,back,1)
                    tot=piece if tot is None else tot+piece
                h,zq=g//2,g%2
                if GL*g-128*t>=0:
                    fold_scr[w,h,zq,zk]=tot
                else:
                    fold_scr[w,h,zq,zk]+=tot
    yield
    for h in range(HEADS):
        for zq in range(WZ):
            for zk in range(WZ):
                f=fold_scr[w,h,zq,zk]
                lo_t=None; hi_t=None
                lane6=lax.broadcasted_iota(jnp.int32,(8,128),1)
                for dw in range(4):
                    part=jnp.concatenate([f[6*dw:6*dw+6],jnp.zeros((2,128),F32)],axis=0)
                    sh=18-6*dw
                    r=pltpu.roll(part,sh,1) if sh else part
                    a=jnp.where(lane6>=sh,r,0.0) if sh>8 else r
                    lo_t=a if lo_t is None else lo_t+a
                    if sh>8:
                        b=jnp.where(lane6<sh-8,r,0.0)
                        hi_t=b if hi_t is None else hi_t+b
                n=(h*WZ+zq)*WZ+zk
                fold_ref[0,w,24*(n//3)+7*(n%3):24*(n//3)+7*(n%3)+6]=lo_t[:6]
                tail_scr[w,8*n:8*n+8]=hi_t
    tail=tail_scr[w,pl.ds(0,24,stride=8),:]
    for hk in range(1,WLAT):
        tail=tail+pltpu.roll(tail_scr[w,pl.ds(hk,24,stride=8),:],10*hk,1)
    row7_scr[w]=tail
    for m in range(3):
        fold_ref[0,w,pl.ds(7*m+6,8,stride=24),:]=row7_scr[w,pl.ds(m,8,stride=3),:]
    yield
    ph=ph_scr[w]; dsc=ds_scr[w]
    ctxT=jnp.concatenate([nn(vT[32*h:32*h+32],ph[:,128*h:128*h+256])[:,16*h:16*h+WTOK] for h in range(HEADS)],axis=0).astype(BF16)
    dqT=jnp.concatenate([nn(kT[32*h:32*h+32],dsc[:,128*h:128*h+256])[:,16*h:16*h+WTOK] for h in range(HEADS)],axis=0).astype(BF16)
    yield
    ctx=nt(eye144,ctxT).astype(BF16)
    dq=nt(eye144,dqT).astype(BF16)
    yield
    dv=nn(ph,dblk).astype(BF16)
    dk=nn(dsc,qblk).astype(BF16)
    o_scr[0,toks]=(x+nn(ctx,wp)).astype(BF16)
    yield
    ng=nt(dq,wq)+nt(dk,wk)+nt(dv,wv)
    g=ng*gain
    br=inv*(g-jnp.mean(g,axis=-1,keepdims=True)-std*jnp.mean(g*std,axis=-1,keepdims=True))
    o_scr[1,toks]=(u.astype(F32)+br).astype(BF16)
    rows=slice(base+w*WTOK,base+(w+1)*WTOK)
    normed_scr[rows]=normed; gq_scr[rows]=dq; gk_scr[rows]=dk; gv_scr[rows]=dv; ctx_scr[rows]=ctx; up_scr[rows]=u
    result.append((jnp.sum(ng*std,axis=0,keepdims=True), jnp.sum(ng,axis=0,keepdims=True)))

def kernel(first, *refs):
    count=2 if first else 4
    ins=refs[:count]
    perm_ref,back_ref,gain_ref,shift_ref,wqkv_ref,wp_ref,bias_ref=refs[count:count+7]
    refs=refs[count+7:]
    if first:
        outs,refs=refs[:2],refs[2:]
        fold_ref,w_ref,ngrad_ref,x_scr,o_scr=refs[:5]
    else:
        w_in,ngrad_in=refs[:2]
        outs,refs=refs[2:6],refs[6:]
        fold_ref,wgrad_ref,x_scr,o_scr,w_ref=refs[:5]
    scr=refs[5:]
    half=slice(0,WTOK); rest=slice(WTOK,2*WTOK)
    for s in range(2):
        if first:
            t=[ins[0][s,half],ins[1][s,half],ins[0][s,rest],ins[1][s,rest]]
        else:
            t=[ref[s] for ref in ins]
        x_scr[s]=nn(perm_ref[...],jnp.concatenate(t,axis=0)).astype(BF16)
    eye=(lax.broadcasted_iota(jnp.int32,(WTOK,WTOK),0)==lax.broadcasted_iota(jnp.int32,(WTOK,WTOK),1)).astype(BF16)
    wqkv=wqkv_ref[...]
    wq,wk,wv=wqkv[:,:C],wqkv[:,C:2*C],wqkv[:,2*C:]
    flip=(lax.broadcasted_iota(jnp.int32,(C,C),0)==lax.broadcasted_iota(jnp.int32,(C,C),1)).astype(BF16)
    wkT,wvT=nt(flip,wk).astype(BF16),nt(flip,wv).astype(BF16)
    gs=[]
    live=[window(w,w,x_scr,o_scr,gain_ref[...],shift_ref[...],wq,wk,wv,wkT,wvT,wp_ref[...],bias_ref,
            fold_ref,*scr,eye,0,gs) for w in range(NW)]
    done=object()
    while live:
        live=[g for g in live if next(g,done) is not done]
    for s in range(2):
        t=nn(back_ref[...],o_scr[s]).astype(BF16)
        if first:
            outs[0][s,half]=t[:WTOK]; outs[1][s,half]=t[WTOK:2*WTOK]
            outs[0][s,rest]=t[2*WTOK:3*WTOK]; outs[1][s,rest]=t[3*WTOK:]
        else:
            for n,ref in enumerate(outs):
                ref[s]=t[WTOK*n:WTOK*(n+1)]
    normed_scr,gq_scr,gk_scr,gv_scr,ctx_scr,up_scr=scr[5:11]
    n=normed_scr[...]
    whole=jnp.concatenate([tn(n,gq_scr[...]),tn(n,gk_scr[...]),tn(n,gv_scr[...]),tn(ctx_scr[...],up_scr[...])],axis=1)
    ng=jnp.concatenate([sum(g[0] for g in gs),sum(g[1] for g in gs),jnp.zeros((6,C),F32)],axis=0)
    if first:
        for t in range(6):
            w_ref[C*t:C*(t+1)]=whole[:,128*t:128*(t+1)]
        ngrad_ref[...]=ng
        return
    for t in range(6):
        w_ref[C*t:C*(t+1)]=whole[:,128*t:128*(t+1)]+w_in[C*t:C*(t+1)]
    ng=ng+ngrad_in[...]
    for r in range(3):
        for t in range(6):
            m=r*6+t
            wgrad_ref[pl.ds((m//9)*64*16+m%9,64,stride=16),:]=w_ref[pl.ds(C*t+r,64,stride=3),:]
    for h in range(2):
        wgrad_ref[pl.ds(h*64*16+9,64,stride=16),:]=jnp.broadcast_to(ng[h:h+1,:128],(64,128))
        wgrad_ref[pl.ds(h*64*16+10,64,stride=16),:]=jnp.broadcast_to(jnp.concatenate([ng[h:h+1,128:],jnp.zeros((1,64),F32)],axis=1),(64,128))

def token_order():
    hot=np.zeros((576,576),np.float32)
    for lev in range(8):
        for w in range(WLON):
            for h in range(WLAT):
                quad=h//3*2+w//6
                hot[(lev*WLON+w)*WLAT+h,quad*WTOK+h%3*48+w%6*8+(lev-1)%8]=1.0
    return hot

def attend(row,parts,weights,vtab,sums=()):
    first=row==1
    full=lambda *s: pl.BlockSpec(s,lambda i:(0,)*len(s))
    tok=4*WTOK
    hot=token_order()
    own=[full(*p.shape) for p in parts]
    wsum=pltpu.VMEM((6*C,128),F32)
    ends=[(6*C,128),(8,C)] if first else [(2*64*16,128)]
    return pl.pallas_call(
        functools.partial(kernel,first),
        grid=(1,),
        in_specs=own+[full(tok,tok)]*2+[full(1,C),full(1,C),full(C,3*C),full(C,C)]
                 +[pl.BlockSpec((1,HEADS,4,WZ,WZ,24,128),lambda i:(row,0,0,0,0,0,0))]+[full(*s.shape) for s in sums],
        out_specs=own+[full(1,4,192,128)]+[full(*s) for s in ends],
        out_shape=[jax.ShapeDtypeStruct(p.shape,BF16) for p in parts]+[jax.ShapeDtypeStruct((1,4,192,128),F32)]
                  +[jax.ShapeDtypeStruct(s,F32) for s in ends],
        scratch_shapes=[pltpu.VMEM((2,tok,C),BF16),pltpu.VMEM((2,tok,C),BF16)]+([] if first else [wsum])
                       +[pltpu.VMEM((NW,WTOK,QP),F32),pltpu.VMEM((NW,WTOK,QP),F32),pltpu.VMEM((NW,WTOK,QP),BF16),pltpu.VMEM((NW,WTOK,QP),BF16),
                        pltpu.VMEM((NW,HEADS,WZ,WZ,24,128),F32)]+[pltpu.VMEM((tok,C),BF16)]*6
                       +[pltpu.VMEM((NW,192,128),F32),pltpu.VMEM((NW,24,128),F32)],
        compiler_params=pltpu.CompilerParams(dimension_semantics=("arbitrary",),vmem_limit_bytes=32*1024*1024),
        cost_estimate=pl.CostEstimate(flops=3*10**9,bytes_accessed=4000000,transcendentals=5*10**5),
        name="attend_first" if first else "attend_last",
    )(*parts,jnp.asarray(hot,BF16),jnp.asarray(hot.T,BF16),*weights,vtab,*sums)

def table_order():
    hot=np.zeros((828,896),np.float32)
    for hq in range(WLAT):
        for hk in range(WLAT):
            for o in range(23):
                i=o*WLAT+hq
                hot[(hq*WLAT+hk)*23+o,128*hk+i if i<128 else 768+10*hk+i-128]=1.0
    return hot

def table_kernel(lat_ref,t_ref,hot_ref,out_ref):
    rows=2*HEADS*4
    row=lax.broadcasted_iota(jnp.int32,(rows,128),0)
    lane=lax.broadcasted_iota(jnp.int32,(rows,128),1)
    low=lane%WLAT<WLAT//2
    edge=(row<rows//2)&(lat_ref[0]==0)
    bottom=row%4==0
    hot=hot_ref[...]
    for zz in range(4):
        t=jnp.concatenate([t_ref[a,h,:,828*zz:828*(zz+1)] for a in range(2) for h in range(HEADS)],axis=0)
        hi=t.astype(BF16); rest=t-hi.astype(F32)
        mid=rest.astype(BF16); lo=(rest-mid.astype(F32)).astype(BF16)
        v=nn(jnp.concatenate([hi,mid,lo],axis=0),hot)
        v=v[:rows]+v[rows:2*rows]+v[2*rows:]
        tail=v[:,768:896]
        for hk in range(WLAT):
            main=v[:,128*hk:128*(hk+1)]
            cut=edge&(low!=(hk<WLAT//2))
            if zz in (1,2): cut=cut|bottom
            for dw in range(4):
                s=18-6*dw
                r=pltpu.roll(main,128-s,1) if s else main
                if s>8:
                    r=jnp.where(lane>=128-s,pltpu.roll(tail,(128-s-10*hk)%128,1),r)
                out_ref[pl.ds(zz*24+dw*WLAT+hk,rows,stride=96),:]=jnp.where(cut,MASKED,r)

def spread_table(earth_bias, lat):
    flat=earth_bias.transpose(0,2,1,3)
    whole=pl.BlockSpec(memory_space=pltpu.VMEM)
    out=pl.pallas_call(
        table_kernel,
        in_specs=[pl.BlockSpec(memory_space=pltpu.SMEM),whole,whole],
        out_specs=whole,
        out_shape=jax.ShapeDtypeStruct((48*96,128),F32),
        compiler_params=pltpu.CompilerParams(vmem_limit_bytes=16*1024*1024),
        cost_estimate=pl.CostEstimate(flops=2*576*828*896,bytes_accessed=5000000,transcendentals=0),
        name="table",
    )(jnp.full((1,),lat,jnp.int32),flat,jnp.asarray(table_order(),BF16))
    return out.reshape(2,HEADS,4,WZ,WZ,24,128)

def unfold_grad(g):
    n=g.shape[0]
    v=jnp.concatenate([g[:,:6],g[:,6,:60].reshape(n,6,10)],axis=-1)
    return v.reshape(n,WLAT,23,WLAT).transpose(0,3,1,2).reshape(n,828)

LON = ("xl", "y", "z")
LAT = ("xh", "c")
ZWIN = 4
GRAD_SCALE = 1.0 / math.sqrt(294912)


def along(block, axis, distance):
    size = lax.axis_size(axis)
    return lax.ppermute(block, axis, [(i, (i + distance) % size) for i in range(size)])


def across(block, lon_step, lat_step):
    lon, lat = lax.axis_size(LON), lax.axis_size(LAT)
    route = [
        (i * lat + j, (i + lon_step) % lon * lat + (j + lat_step) % lat)
        for i in range(lon)
        for j in range(lat)
    ]
    return lax.ppermute(block, LON + LAT, route)


def pack_kernel(places, x_ref, u_ref, *refs):
    count = len(places)
    outs, held, sems = refs[:count], refs[count : 2 * count], refs[-1]
    arrive, leave = [], []
    for n, (rows, cols) in enumerate(places):
        for s, src in enumerate((x_ref, u_ref)):
            arrive.append(pltpu.make_async_copy(src.at[rows, cols], held[n].at[s], sems.at[0, n, s]))
            leave.append(pltpu.make_async_copy(held[n].at[s], outs[n].at[s], sems.at[1, n, s]))
    for copy in arrive:
        copy.start()
    for first, second in zip(arrive, leave):
        first.wait()
        second.start()
    for copy in leave:
        copy.wait()


def pack(x, u, places):
    shapes = [(2, rows.size, cols.size, 8, C) for rows, cols in places]
    outs = pl.pallas_call(
        functools.partial(pack_kernel, places),
        in_specs=[pl.BlockSpec(memory_space=pl.ANY)] * 2,
        out_specs=[pl.BlockSpec(memory_space=pl.ANY)] * len(places),
        out_shape=[jax.ShapeDtypeStruct(s, BF16) for s in shapes],
        scratch_shapes=[pltpu.VMEM(s, BF16) for s in shapes] + [pltpu.SemaphoreType.DMA((2, len(places), 2))],
        compiler_params=pltpu.CompilerParams(vmem_limit_bytes=60 * 1024 * 1024),
        name="pack",
    )(x, u)
    return [p.reshape(2, -1, C) for p in outs]


def on_device(air_state, cotangent, norm_gain, norm_shift, qkv_weight, proj_weight, earth_bias):
    half = WLON // 2
    west, east = pl.ds(0, half), pl.ds(half, half)
    upper, middle, lower = pl.ds(0, WLAT // 2), pl.ds(WLAT // 2, WLAT), pl.ds(3 * WLAT // 2, WLAT // 2)
    x, u = air_state.transpose(1, 2, 0, 3), cotangent.transpose(1, 2, 0, 3)
    sent_left, sent_corner, sent_above, sent_bottom, own_upper, own_middle = pack(
        x, u, ((middle, east), (lower, west), (lower, east), (upper, west), (upper, east), (middle, west))
    )
    left = across(sent_left, 1, 0)
    corner = across(sent_corner, -1, 1)
    above = across(sent_above, 0, 1)
    bottom = across(sent_bottom, -1, 0)
    table = spread_table(earth_bias, lax.axis_index(LAT))
    weights = (norm_gain.reshape(1, C), norm_shift.reshape(1, C), qkv_weight, proj_weight)
    left, own_middle, fold_first, *sums = attend(1, [left, own_middle], weights, table)
    left = across(left, -1, 0)
    above, corner, own_upper, bottom, fold_last, wgrad = attend(0, [above, corner, own_upper, bottom], weights, table, sums)
    fold = jnp.concatenate((fold_last, fold_first))
    wgrad = wgrad.reshape(2, 64, 16, 128)[:, :, :11].astype(BF16)

    corner = across(corner, 1, -1)
    above = across(above, 0, -1)
    bottom = across(bottom, 1, 0)

    core = lax.axis_index("c")
    kept = lax.dynamic_index_in_dim(wgrad, core, 0, keepdims=False)
    other = along(lax.dynamic_index_in_dim(wgrad, 1 - core, 0, keepdims=False), "c", 1)
    wpart = (kept.astype(F32) + other.astype(F32)).astype(BF16)
    payload = jnp.concatenate((fold.reshape(64, 24, 128)[:, :21].astype(BF16), wpart), axis=1)
    parts = lax.all_to_all(payload, LON, 0, 0, tiled=True)
    mine = jnp.sum(parts.astype(F32), axis=0)
    wsum = mine[21:]
    wsum = (wsum + along(wsum, "xh", 1)) * GRAD_SCALE
    bsum = unfold_grad(mine[:21].reshape(3, 7, 128)).reshape(-1)
    bsum = jnp.pad(bsum, (0, 20 * 128 - bsum.shape[0])).reshape(20, 128)
    shard = jnp.concatenate((bsum, wsum), axis=0).astype(BF16)
    shard = jnp.pad(shard, ((0, 1), (0, 0)))
    shard, left, bottom, corner, above = lax.optimization_barrier((shard, left, bottom, corner, above))
    column = lax.all_to_all(jnp.broadcast_to(shard, (8,) + shard.shape), "z", 0, 0, tiled=True)
    spread = lax.all_to_all(jnp.broadcast_to(column, (8,) + column.shape), ("xl", "y"), 0, 0, tiled=True)
    spread = spread.reshape((64,) + shard.shape)
    bias_grad = spread[:, :20].reshape(64, 2560)[:, :2484].reshape(2, ZWIN, HEADS, POSITIONS)
    whalf = spread[:, 20:29]
    nhalf = wsum[9:11]
    wother = along(whalf, "c", 1)
    nother = along(nhalf, "c", 1)
    first = core == 0
    w0 = jnp.where(first, whalf, wother)
    w1 = jnp.where(first, wother, whalf)
    wall = jnp.concatenate((w0, w1), axis=1).reshape(C, 4 * C).astype(F32)
    gain_grad = jnp.where(first, nhalf, nother).reshape(256)[:C]
    shift_grad = jnp.where(first, nother, nhalf).reshape(256)[:C]

    def joined(left, right):
        return jnp.concatenate([t.reshape(2, -1, half, 8, C) for t in (left, right)], axis=2)

    grid = jnp.concatenate((joined(bottom, own_upper), joined(own_middle, left), joined(corner, above)), axis=1)
    both = grid.transpose(0, 3, 1, 2, 4)

    return both[0], both[1], wall[:, : 3 * C], wall[:, 3 * C :], gain_grad, shift_grad, bias_grad


def solution(mesh):
    fine = Mesh(mesh.devices.reshape(2, 4, 8, 2, 2), LON + LAT)
    token = P(None, LAT, LON, None)
    table = P(LAT, None, None, None)
    return jax.shard_map(
        on_device,
        mesh=fine,
        in_specs=(token, token, P(), P(), P(), P(), table),
        out_specs=(token, token, P(), P(), P(), P(), table),
        check_vma=False,
    )
```
